256 devices in a mesh: prow: 8 (over z_lo, y), pcol: 32 (over z_hi, x, core).
Axes of the slice: x: 4, y: 4, z: 8 (z_hi: 4, z_lo: 2; z = z_hi * 2 + z_lo), core: 2. Of those that a mesh axis runs over, the one named last changes fastest.
Arguments:
- matrix: float32 [8192, 24576], P('prow', 'pcol'), may hold values from -9 to 9, as said below
- pivot_rows: int32 [128], replicated, may hold values from 128 to 8191, as said below
Outputs:
- factored: float32 [8192, 24576], P('prow', 'pcol')
The draws below stay inside these ranges and needn't reach their ends.
Inputs may be any that keep to these rules, and one draw needn't show every extreme that they name: `matrix`: columns 0 to 127 hold a factored panel: in global rows 0 to 127 the strictly lower part is the unit lower factor and the rest the upper factor; in all other rows the multipliers, of magnitude at most 1. `pivot_rows`: 128 distinct global rows, none of them among rows 0 to 127.
All inputs are finite; a program needn't handle non-finite values.
Results may differ from the reference program's by a relative error of at most 0.000065.
Values sent between devices are 32-bit elements; how exact they have to be, the bound alone decides.
No kernel may reach another device: no remote copies, remote signals or barrier semaphores. Data moves between devices by JAX's collectives and lax.ppermute only.
A program may use at most 64 MiB of HBM per device.

```python
import jax
import jax.numpy as jnp
from jax import lax

NB = 128
ROWS_DEV = 1024
COLS_DEV = 768
M = 8192
N = 24576
N_PROW = 8
N_PCOL = 32


def draw_matrix(key, part):
    key = jax.random.fold_in(key, 11)
    key_base = jax.random.fold_in(key, 0)
    key_panel = jax.random.fold_in(key, 1)
    key_lower = jax.random.fold_in(key, 3)
    row_ids = jnp.arange(M)[:, None]
    col_ids = jnp.arange(N)[None, :]
    global_row = row_ids % ROWS_DEV // NB * NB * N_PROW + row_ids // ROWS_DEV * NB + row_ids % NB
    global_col = col_ids % COLS_DEV // NB * NB * N_PCOL + col_ids // COLS_DEV * NB + col_ids % NB
    base = jnp.clip(jax.random.normal(key_base, (M, N), jnp.float32), -8.0, 8.0)
    multipliers = jax.random.uniform(key_panel, (M, N), jnp.float32, -1.0, 1.0)
    factor_low = jax.random.uniform(key_lower, (M, N), jnp.float32, -0.1, 0.1)
    in_panel = global_col < NB
    in_top = global_row < NB
    below = global_row > global_col
    panel_values = jnp.where(in_top, jnp.where(below, factor_low, base), multipliers)
    return jnp.where(in_panel, panel_values, base).astype(jnp.float32)


def draw_pivot_rows(key, part):
    key = jax.random.fold_in(key, 23)
    key_perm, key_first, key_second = jax.random.split(key, 3)
    inner = NB + 1 + jax.random.permutation(key_perm, M - NB - 2)[:NB]
    first = jax.random.randint(key_first, (), 0, NB)
    second = (first + 1 + jax.random.randint(key_second, (), 0, NB - 1)) % NB
    inner = inner.at[first].set(NB)
    inner = inner.at[second].set(M - 1)
    return inner.astype(jnp.int32)


def setup_inputs(seed: int = 0) -> dict:
    key_list = jax.random.split(jax.random.key(seed), 3)
    matrix = draw_matrix(jax.random.fold_in(key_list[2], 71), 0)
    pivot_rows = draw_pivot_rows(jax.random.fold_in(key_list[2], 71), 0)
    return dict(matrix=matrix, pivot_rows=pivot_rows)


def stored_rows(global_row):
    return global_row // NB % N_PROW * ROWS_DEV + global_row // (NB * N_PROW) * NB + global_row % NB

def reference(matrix, pivot_rows):
    places = stored_rows(pivot_rows).astype(jnp.int32)
    panel_block = matrix[:, :NB]
    lower_block = jnp.tril(panel_block[:NB], -1) + jnp.eye(NB, dtype=matrix.dtype)
    picked = jnp.take(matrix, places, axis=0)
    solved = jax.scipy.linalg.solve_triangular(lower_block, picked, lower=True, unit_diagonal=True)
    product = jnp.dot(panel_block, solved, precision=lax.Precision.HIGHEST)
    displaced = matrix[:NB] - jnp.take(product, places, axis=0)
    factored = matrix - product
    factored = factored.at[places].set(displaced)
    factored = factored.at[:NB].set(solved)
    factored = factored.at[:, :NB].set(panel_block)
    return factored
```

```python
import functools

import jax
import jax.numpy as jnp
from jax import lax
from jax.experimental import pallas as pl
from jax.experimental.pallas import tpu as pltpu
from jax.sharding import Mesh, PartitionSpec as P

NB = 128
EXACT = lax.Precision.HIGHEST
ROWS = ("zl", "y")
COLS = ("zh", "x", "c")
N_Y, N_X, N_ZH, N_C = 4, 4, 4, 2
N_PROW = 8


def prow_id(zl, y):
    return zl * N_Y + y


def pcol_id(zh, x, c):
    return (zh * N_X + x) * N_C + c


def owned_row(pivot, my_row):
    is_owned = ((pivot >> 7) & (N_PROW - 1)) == my_row
    return is_owned, ((pivot >> 10) << 7) + (pivot & (NB - 1))


def pick_kernel(pivots, my_row, matrix, out):
    cols = matrix.shape[1]
    step = NB // N_PROW
    on_top = my_row[0] == 0

    def body(j, _):
        for i in range(step):
            is_owned, row = owned_row(pivots[j * step + i], my_row[0])
            got = matrix[pl.ds(jnp.where(is_owned, row, 0), 1), :]
            out[j, pl.ds(i, 1), :] = jnp.where(is_owned, got, 0.0)
        top = matrix[pl.ds(pl.multiple_of(j * step, step), step), :]
        out[j, step:, :] = jnp.where(on_top, top, 0.0)
        return 0

    lax.fori_loop(0, N_PROW, body, 0)


def pick(pivots, my_row, matrix):
    cols = matrix.shape[1]
    return pl.pallas_call(
        pick_kernel,
        out_shape=jax.ShapeDtypeStruct((N_PROW, 2 * NB // N_PROW, cols), jnp.float32),
        grid_spec=pltpu.PrefetchScalarGridSpec(
            num_scalar_prefetch=2,
            grid=(1,),
            in_specs=[pl.BlockSpec(matrix.shape, lambda i, *_: (0, 0))],
            out_specs=pl.BlockSpec(
                (N_PROW, 2 * NB // N_PROW, cols), lambda i, *_: (0, 0, 0)
            ),
        ),
        compiler_params=pltpu.CompilerParams(vmem_limit_bytes=32 << 20),
        name="pick",
    )(pivots, my_row, matrix)


def invert_kernel(block, out):
    rows = lax.broadcasted_iota(jnp.int32, (NB, NB), 0)
    cols = lax.broadcasted_iota(jnp.int32, (NB, NB), 1)
    lower = block[...]
    inverse = jnp.where(rows == cols, 1.0, 0.0)
    size = 1
    while size < NB:
        shift = size.bit_length()
        same = (rows >> shift) == (cols >> shift)
        below = ((rows & size) != 0) & ((cols & size) == 0)
        part = jnp.where(same & below, lower, 0.0)
        if size == 1:
            inverse = inverse - part
        else:
            half = jnp.dot(part, inverse, precision=EXACT, preferred_element_type=jnp.float32)
            inverse = inverse - jnp.dot(
                inverse, half, precision=EXACT, preferred_element_type=jnp.float32
            )
        size *= 2
    out[...] = inverse


def invert(block):
    return pl.pallas_call(
        invert_kernel,
        out_shape=jax.ShapeDtypeStruct((NB, NB), jnp.float32),
        name="invert",
    )(block)


def solve_kernel(pivots, my_row, matrix, inverse, rows, swapped, solved):
    step = NB // N_PROW
    picked = rows[:, :step, :].reshape(NB, rows.shape[-1])
    solved[...] = jnp.dot(
        inverse[...], picked, precision=EXACT, preferred_element_type=jnp.float32
    )
    swapped[...] = matrix[...]

    def body(j, _):
        for i in range(step):
            is_owned, row = owned_row(pivots[j * step + i], my_row[0])

            @pl.when(is_owned)
            def _():
                swapped[pl.ds(row, 1), :] = rows[j, pl.ds(step + i, 1), :]

        return 0

    lax.fori_loop(0, N_PROW, body, 0)


def solve(pivots, my_row, matrix, inverse, rows):
    whole = lambda a: pl.BlockSpec(a.shape, lambda i, *_: (0,) * a.ndim)
    return pl.pallas_call(
        solve_kernel,
        out_shape=(
            jax.ShapeDtypeStruct(matrix.shape, jnp.float32),
            jax.ShapeDtypeStruct((NB, matrix.shape[1]), jnp.float32),
        ),
        grid_spec=pltpu.PrefetchScalarGridSpec(
            num_scalar_prefetch=2,
            grid=(1,),
            in_specs=[whole(matrix), whole(inverse), whole(rows)],
            out_specs=(
                pl.BlockSpec(matrix.shape, lambda i, *_: (0, 0)),
                pl.BlockSpec((NB, matrix.shape[1]), lambda i, *_: (0, 0)),
            ),
        ),
        compiler_params=pltpu.CompilerParams(vmem_limit_bytes=48 << 20),
        name="solve",
    )(pivots, my_row, matrix, inverse, rows)


def update_kernel(place, panel, solved, swapped, out):
    step = pl.program_id(0)
    piece = panel[0]
    out[...] = swapped[...] - jnp.dot(
        piece, solved[...], precision=EXACT, preferred_element_type=jnp.float32
    )
    first = ((place[1] + N_X - step) & (N_X - 1)) == 0

    @pl.when((place[0] == 0) & first)
    def _():
        out[:NB, :] = solved[...]

    @pl.when(place[2] == 0)
    def _():
        out[:, :NB] = piece


def update(place, panel, solved, swapped):
    parts, height, _ = panel.shape
    cols = swapped.shape[1]
    block = lambda i, place: ((place[1] + N_X - i) & (N_X - 1), 0)
    return pl.pallas_call(
        update_kernel,
        out_shape=jax.ShapeDtypeStruct(swapped.shape, jnp.float32),
        grid_spec=pltpu.PrefetchScalarGridSpec(
            num_scalar_prefetch=1,
            grid=(parts,),
            in_specs=[
                pl.BlockSpec((1, height, NB), lambda i, place: (i, 0, 0)),
                pl.BlockSpec(solved.shape, lambda i, place: (0, 0)),
                pl.BlockSpec((height, cols), block),
            ],
            out_specs=pl.BlockSpec((height, cols), block),
        ),
        compiler_params=pltpu.CompilerParams(vmem_limit_bytes=48 << 20),
        name="update",
    )(place, panel, solved, swapped)


def local(matrix, pivot_rows):
    height = matrix.shape[0] // N_X
    zl, y = lax.axis_index("zl"), lax.axis_index("y")
    zh, x, c = (lax.axis_index(name) for name in COLS)
    my_row = prow_id(zl, y)
    my_col = pcol_id(zh, x, c)
    row_arg = my_row.reshape(1).astype(jnp.int32)
    place = jnp.stack([my_row, x, my_col]).astype(jnp.int32)

    top = matrix[:NB, :NB]
    lower = top
    origin = my_row == 0
    for pairs in (
        [(prow_id(0, 0), prow_id(1, 0))],
        [(prow_id(a, 0), prow_id(a, 1)) for a in (0, 1)],
        [(prow_id(a, b), prow_id(a, (3, 2)[b])) for a in (0, 1) for b in (0, 1)],
    ):
        whole = [(s * 32, t * 32) for s, t in pairs]
        got = lax.ppermute(lower, ROWS + COLS, whole)
        is_target = functools.reduce(
            jnp.logical_or, [my_row == t for _, t in pairs], jnp.bool_(False)
        )
        lower = jnp.where(is_target, got, lower)

    quarter = matrix[:height, :NB]
    for k in range(1, N_X):
        piece = matrix[k * height : (k + 1) * height, :NB]
        got = lax.ppermute(piece, COLS, [(0, pcol_id(0, k, 0))])
        quarter = jnp.where(x == k, got, quarter)

    sent = pick(pivot_rows, row_arg, matrix)
    got = lax.all_to_all(sent, ROWS, 0, 0)
    mine = jnp.sum(got, axis=0)
    rows = lax.all_to_all(
        jnp.broadcast_to(mine[None], (N_PROW,) + mine.shape), ROWS, 0, 0
    )

    held = jnp.concatenate([quarter, lower], axis=0)
    down = held
    for k in range(1, N_ZH):
        got = lax.ppermute(
            held, COLS, [(pcol_id(0, a, 0), pcol_id(k, a, 0)) for a in range(N_X)]
        )
        down = jnp.where(zh == k, got, down)

    pieces = [down[:height]]
    lower = down[height:]
    for k in range(1, N_X):
        got = lax.ppermute(
            down,
            COLS,
            [
                (pcol_id(b, a, 0), pcol_id(b, (a + k) % N_X, 0))
                for a in range(N_X)
                for b in range(N_ZH)
            ],
        )
        pieces.append(got[:height])
        lower = jnp.where(x == k, got[height:], lower)

    held = jnp.concatenate(pieces + [lower], axis=0)
    got = lax.ppermute(
        held,
        COLS,
        [(pcol_id(b, a, 0), pcol_id(b, a, 1)) for a in range(N_X) for b in range(N_ZH)],
    )
    held = jnp.where(c == 1, got, held)
    panel = held[: N_X * height].reshape(N_X, height, NB)
    inverse = invert(held[N_X * height :])
    swapped, solved = solve(pivot_rows, row_arg, matrix, inverse, rows)
    return update(place, panel, solved, swapped)


def solution(mesh):
    fine = Mesh(mesh.devices.reshape(2, N_Y, N_ZH, N_X, N_C), ROWS + COLS)
    placed = (P(ROWS, COLS), P())
    return jax.shard_map(
        local, mesh=fine, in_specs=placed, out_specs=P(ROWS, COLS), check_vma=False
    )
```

```python
import functools

import jax
import jax.numpy as jnp
from jax import lax
from jax.experimental import pallas as pl
from jax.experimental.pallas import tpu as pltpu
from jax.sharding import Mesh, PartitionSpec as P

NB = 128
EXACT = lax.Precision.HIGHEST
ROWS = ("zl", "y")
COLS = ("zh", "x", "c")
N_Y, N_X, N_ZH, N_C = 4, 4, 4, 2
N_PROW, N_PCOL = 8, 32
N_PART = 4
STEP = NB // N_PROW
SLOTS = 32
BLOCK = 16
PLAN_ROWS = 8

VMEM = pl.BlockSpec(memory_space=pltpu.VMEM)
SMEM = pl.BlockSpec(memory_space=pltpu.SMEM)
ANY = pl.BlockSpec(memory_space=pl.ANY)


SMALL = pltpu.CompilerParams(vmem_limit_bytes=12 << 20)
LARGE = pltpu.CompilerParams(vmem_limit_bytes=56 << 20)


def prow_id(zl, y):
    return zl * N_Y + y


def pcol_id(zh, x, c):
    return (zh * N_X + x) * N_C + c


def my_place():
    row = prow_id(lax.axis_index("zl"), lax.axis_index("y"))
    col = pcol_id(*(lax.axis_index(name) for name in COLS))
    return row, col


NEAR = (1, 0, 3, 2)
FAR = (3, 2, 1, 0)


def send_cols(value, pairs):
    return lax.ppermute(value, COLS, [(pcol_id(*s), pcol_id(*t)) for s, t in pairs])


def send_rows(value, pairs, cols=range(N_PCOL)):
    pairs = [(prow_id(*s) * N_PCOL + q, prow_id(*t) * N_PCOL + q) for s, t in pairs for q in cols]
    return lax.ppermute(value, ROWS + COLS, pairs)


def after(value, first):
    return lax.optimization_barrier((value, first))[0]


def owned_row(pivot, my_row):
    is_owned = ((pivot >> 7) & (N_PROW - 1)) == my_row
    return is_owned, jnp.where(is_owned, ((pivot >> 10) << 7) + (pivot & (NB - 1)), 0)


def to_column(row):
    size = row.shape[1]
    rows = lax.broadcasted_iota(jnp.int32, (size, size), 0)
    cols = lax.broadcasted_iota(jnp.int32, (size, size), 1)
    return jnp.sum(jnp.where(rows == cols, row, 0.0), axis=1, keepdims=True)


def ranks_of(pivots):
    owner = ((pivots >> 7) & (N_PROW - 1)).astype(jnp.float32)
    rows = lax.broadcasted_iota(jnp.int32, (NB, NB), 0)
    cols = lax.broadcasted_iota(jnp.int32, (NB, NB), 1)
    before = (to_column(owner) == owner) & (rows < cols)
    return jnp.sum(jnp.where(before, 1.0, 0.0), axis=0, keepdims=True)


def plan_kernel(pivots, out):
    my_row, _ = my_place()
    ranks = ranks_of(pivots[...])
    owner = (pivots[...] >> 7) & (N_PROW - 1)
    is_owned, row = owned_row(pivots[...], my_row)
    rank = to_column(jnp.where(is_owned, ranks, -1.0))
    wanted = lax.broadcasted_iota(jnp.int32, (NB, NB), 1).astype(jnp.float32)
    rows = jnp.where(rank == wanted, to_column(row.astype(jnp.float32)), 0.0)
    count = jnp.sum(is_owned.astype(jnp.float32), axis=1, keepdims=True)
    most = jnp.max(ranks, axis=1, keepdims=True) + 1.0
    out[...] = jnp.zeros_like(out)
    out[0:1, :] = owner * NB + ranks.astype(jnp.int32)
    out[1:2, :] = jnp.sum(rows, axis=0, keepdims=True).astype(jnp.int32)
    out[2:3, :] = jnp.broadcast_to(count, (1, NB)).astype(jnp.int32)
    out[3:4, :] = jnp.broadcast_to(most, (1, NB)).astype(jnp.int32)


def make_plan(pivots):
    return pl.pallas_call(
        plan_kernel,
        out_shape=jax.ShapeDtypeStruct((PLAN_ROWS, NB), jnp.int32),
        in_specs=[VMEM],
        out_specs=VMEM,
        compiler_params=SMALL,
        cost_estimate=pl.CostEstimate(flops=0, bytes_accessed=3 << 20, transcendentals=0),
        name="plan",
    )(pivots)


def pack_kernel(turn, plan_hbm, matrix, out, plan, held, top, moved, sems, row_sems, out_sems):
    my_row, _ = my_place()
    on_top = my_row == 0
    load = pltpu.make_async_copy(plan_hbm, plan, sems.at[0])
    load_top = pltpu.make_async_copy(matrix.at[pl.ds(0, NB), :], top, sems.at[1])
    load.start()

    @pl.when(on_top)
    def _():
        load_top.start()

    load.wait()
    first = turn[0] * SLOTS
    copies = [
        pltpu.make_async_copy(
            matrix.at[pl.ds(plan[1, first + i], 1), :], held.at[pl.ds(i, 1), :], row_sems.at[i]
        )
        for i in range(SLOTS)
    ]
    for copy in copies:
        copy.start()

    def held_copy(j):
        return pltpu.make_async_copy(held, out.at[j, pl.ds(0, SLOTS), :], out_sems.at[j])

    def moved_copy(j):
        return pltpu.make_async_copy(
            moved.at[pl.ds(j * SLOTS, SLOTS), :],
            out.at[j, pl.ds(SLOTS, SLOTS), :],
            out_sems.at[N_PROW + j],
        )

    @pl.when(on_top)
    def _():
        load_top.wait()

        def move(j, _):
            for i in range(8):
                entry = plan[0, j * 8 + i]
                rank = entry & (NB - 1)
                place = ((entry >> 7) << 5) + (rank & (SLOTS - 1))
                place = jnp.where((rank >> 5) == turn[0], place, N_PROW * SLOTS)
                moved[pl.ds(place, 1), :] = top[pl.ds(j * 8 + i, 1), :]
            return 0

        lax.fori_loop(0, NB // 8, move, 0)
        for j in range(N_PROW):
            moved_copy(j).start()

    for copy in copies:
        copy.wait()
    for j in range(N_PROW):
        held_copy(j).start()

    @pl.when(on_top)
    def _():
        for j in range(N_PROW):
            moved_copy(j).wait()

    for j in range(N_PROW):
        held_copy(j).wait()


def pack(turn, plan, matrix):
    cols = matrix.shape[1]
    return pl.pallas_call(
        pack_kernel,
        out_shape=jax.ShapeDtypeStruct((N_PROW, 2 * SLOTS, cols), jnp.float32),
        in_specs=[SMEM, ANY, ANY],
        out_specs=ANY,
        scratch_shapes=[
            pltpu.SMEM((PLAN_ROWS, NB), jnp.int32),
            pltpu.VMEM((SLOTS, cols), jnp.float32),
            pltpu.VMEM((NB, cols), jnp.float32),
            pltpu.VMEM(((N_PROW + 1) * SLOTS, cols), jnp.float32),
            pltpu.SemaphoreType.DMA((2,)),
            pltpu.SemaphoreType.DMA((SLOTS,)),
            pltpu.SemaphoreType.DMA((2 * N_PROW,)),
        ],
        compiler_params=LARGE,
        cost_estimate=pl.CostEstimate(flops=0, bytes_accessed=6 << 20, transcendentals=0),
        name="pack",
    )(turn, plan, matrix)


def split(value):
    first = value.astype(jnp.bfloat16)
    rest = value - first.astype(jnp.float32)
    second = rest.astype(jnp.bfloat16)
    third = (rest - second.astype(jnp.float32)).astype(jnp.bfloat16)
    return first, second, third


def exact_dot(a, b):
    a1, a2, a3 = split(a)
    b1, b2, b3 = split(b)
    product = functools.partial(jnp.dot, preferred_element_type=jnp.float32)
    lead = jnp.concatenate([a1, a2], axis=1)
    total = product(jnp.concatenate([a1, a3], axis=1), jnp.concatenate([b3, b1], axis=0))
    total = total + product(lead, jnp.concatenate([b2, b2], axis=0))
    return total + product(lead, jnp.concatenate([b1, b1], axis=0))


def inverse_of(lower):
    rows = lax.broadcasted_iota(jnp.int32, (NB, NB), 0)
    cols = lax.broadcasted_iota(jnp.int32, (NB, NB), 1)
    block_bits = BLOCK.bit_length() - 1
    offset = cols - ((rows >> block_bits) << block_bits)
    lower = jnp.where(rows > cols, lower, 0.0)
    inverse = jnp.where(rows == cols, 1.0, 0.0).reshape(NB // BLOCK, BLOCK, NB)
    for j in range(BLOCK - 1):
        column = jnp.sum(jnp.where(offset == j, lower, 0.0), axis=1, keepdims=True)
        column = column.reshape(NB // BLOCK, BLOCK, 1)
        inverse = inverse - column * inverse[:, j : j + 1, :]
    inverse = inverse.reshape(NB, NB)
    size = BLOCK
    while size < NB:
        shift = size.bit_length()
        same = (rows >> shift) == (cols >> shift)
        below = ((rows & size) != 0) & ((cols & size) == 0)
        part = jnp.where(same & below, lower, 0.0)
        inverse = inverse - exact_dot(inverse, exact_dot(part, inverse))
        size *= 2
    return inverse


def weigh_kernel(block, panel_hbm, first, second, other, panel, sem):
    my_row, my_col = my_place()

    @pl.when(my_col == 0)
    def _():
        copy = pltpu.make_async_copy(panel_hbm, panel, sem)
        copy.start()
        inverse = inverse_of(block[...])
        copy.wait()
        start = 0
        for out in (first, second, other):
            out[...] = exact_dot(panel[start : start + out.shape[0], :], inverse)
            start += out.shape[0]

        @pl.when(my_row == 0)
        def _():
            first[:NB, :] = -inverse


def weigh(block, panel):
    height = panel.shape[0]
    quarter = jax.ShapeDtypeStruct((height // 4, NB), jnp.float32)
    half = jax.ShapeDtypeStruct((height // 2, NB), jnp.float32)
    return pl.pallas_call(
        weigh_kernel,
        out_shape=(quarter, quarter, half),
        in_specs=[VMEM, ANY],
        out_specs=(VMEM, VMEM, VMEM),
        scratch_shapes=[pltpu.VMEM((height, NB), jnp.float32), pltpu.SemaphoreType.DMA],
        compiler_params=SMALL,
        name="weigh",
    )(block, panel)


def prepare_kernel(plan_hbm, rows, rest, matrix, base, factors, picked, own, plan, sems):
    my_row, my_col = my_place()
    load = pltpu.make_async_copy(plan_hbm, plan, sems.at[0])
    whole = pltpu.make_async_copy(matrix, base, sems.at[1])
    load.start()
    whole.start()
    load.wait()

    def find(j, _):
        for i in range(8):
            k = j * 8 + i
            entry = plan[0, k]
            place = entry & (SLOTS - 1)
            picked[pl.ds(k, 1), :] = rows[entry >> 7, pl.ds(place, 1), :]
        return 0

    lax.fori_loop(0, NB // 8, find, 0)

    def fetch(turn, source, place, target):
        copy = pltpu.make_async_copy(
            rest.at[turn - 1, source, pl.ds(place, 1), :], target, sems.at[0]
        )
        copy.start()
        copy.wait()

    @pl.when(plan[3, 0] > SLOTS)
    def _():
        def find_late(k, _):
            entry = plan[0, k]
            rank = entry & (NB - 1)

            @pl.when(rank >= SLOTS)
            def _():
                fetch(rank >> 5, entry >> 7, rank & (SLOTS - 1), picked.at[pl.ds(k, 1), :])

            return 0

        lax.fori_loop(0, NB, find_late, 0)

    first, second, third = split(picked[...])
    factors[0, :NB, :] = first
    factors[0, NB:, :] = first
    factors[1, :NB, :] = second
    factors[1, NB:, :] = second
    factors[2, :NB, :] = third
    factors[2, NB:, :] = first
    whole.wait()

    @pl.when(my_col == 0)
    def _():
        own[...] = base[:, :NB]

    def swap(i, _):
        base[pl.ds(plan[1, i], 1), :] = rows[0, pl.ds(SLOTS + i, 1), :]
        return 0

    lax.fori_loop(0, jnp.minimum(plan[2, 0], SLOTS), swap, 0)

    def swap_late(i, _):
        place = SLOTS + (i & (SLOTS - 1))
        fetch(i >> 5, 0, place, base.at[pl.ds(plan[1, i], 1), :])
        return 0

    lax.fori_loop(SLOTS, jnp.maximum(plan[2, 0], SLOTS), swap_late, 0)

    @pl.when(my_row == 0)
    def _():
        base[:NB, :] = jnp.zeros((NB, base.shape[1]), jnp.float32)

    @pl.when(my_col == 0)
    def _():
        base[:, :NB] = own[...]
        factors[:, :, :NB] = jnp.zeros((3, 2 * NB, NB), jnp.bfloat16)


def prepare(plan, rows, rest, matrix):
    height, cols = matrix.shape
    return pl.pallas_call(
        prepare_kernel,
        out_shape=(
            jax.ShapeDtypeStruct(matrix.shape, jnp.float32),
            jax.ShapeDtypeStruct((3, 2 * NB, cols), jnp.bfloat16),
        ),
        in_specs=[ANY, VMEM, ANY, ANY],
        out_specs=(VMEM, VMEM),
        scratch_shapes=[
            pltpu.VMEM((NB, cols), jnp.float32),
            pltpu.VMEM((height, NB), jnp.float32),
            pltpu.SMEM((PLAN_ROWS, NB), jnp.int32),
            pltpu.SemaphoreType.DMA((2,)),
        ],
        compiler_params=SMALL,
        cost_estimate=pl.CostEstimate(flops=0, bytes_accessed=9 << 20, transcendentals=0),
        name="prepare",
    )(plan, rows, rest, matrix)


def holdings():
    x, c = lax.axis_index("x"), lax.axis_index("c")
    bits = ((x == 1) | (x == 2)).astype(jnp.int32), (x >= 2).astype(jnp.int32)
    mine = jnp.where(c == 0, bits[0], bits[1])
    other = jnp.where(c == 0, bits[1], bits[0])
    return c, mine, other


def update_kernel(late, mine, theirs, factors, base, *refs):
    out, buffer, sems = refs[-3:]
    core, my_bit, other_bit = holdings()
    height = mine.shape[0]
    quarters = (2 * core + (my_bit ^ late), 2 * (1 - core) + (other_bit ^ late))
    copies = []
    for s, (piece, quarter) in enumerate(zip((mine, theirs), quarters)):
        start = pl.multiple_of(quarter * height, height)
        first, second, third = split(piece[...])
        lead = jnp.concatenate([first, second], axis=1)
        tail = jnp.concatenate([first, third], axis=1)
        product = functools.partial(jnp.dot, preferred_element_type=jnp.float32)
        total = product(tail, factors[2]) + product(lead, factors[1]) + product(lead, factors[0])
        buffer[s] = base[pl.ds(start, height), :] - total
        copy = pltpu.make_async_copy(buffer.at[s], out.at[pl.ds(start, height), :], sems.at[s])
        copy.start()
        copies.append(copy)
    for copy in copies:
        copy.wait()


def update(late, mine, theirs, factors, base, done):
    height, cols = mine.shape[0], base.shape[1]
    extra = [] if done is None else [done]
    return pl.pallas_call(
        functools.partial(update_kernel, late),
        out_shape=jax.ShapeDtypeStruct(base.shape, jnp.float32),
        in_specs=[VMEM] * 4 + [ANY] * len(extra),
        out_specs=ANY,
        scratch_shapes=[
            pltpu.VMEM((2, height, cols), jnp.float32),
            pltpu.SemaphoreType.DMA((2,)),
        ],
        input_output_aliases={4: 0} if extra else {},
        compiler_params=SMALL,
        cost_estimate=pl.CostEstimate(flops=0, bytes_accessed=4 << 20, transcendentals=0),
        name="update",
    )(mine, theirs, factors, base, *extra)


def blank_kernel(out):
    pass


def blank(shape):
    return pl.pallas_call(
        blank_kernel,
        out_shape=jax.ShapeDtypeStruct(shape, jnp.float32),
        out_specs=ANY,
        compiler_params=SMALL,
        name="blank",
    )()


def later_rounds(plan, matrix):
    most = plan[3, 0]

    def body(state):
        turn, rest = state
        sent = pack(turn.reshape(1), plan, matrix)
        got = lax.all_to_all(sent, ROWS, 0, 0)
        return turn + 1, lax.dynamic_update_slice(rest, got[None], (turn - 1, 0, 0, 0))

    rest = blank((NB // SLOTS - 1, N_PROW, 2 * SLOTS, matrix.shape[1]))
    return lax.while_loop(lambda state: state[0] * SLOTS < most, body, (jnp.int32(1), rest))[1]


def local(matrix, pivot_rows):
    zh, x, c = (lax.axis_index(name) for name in COLS)
    zl, y = (lax.axis_index(name) for name in ROWS)
    panel = lax.optimization_barrier(matrix[:, :NB])
    lower = panel[:NB]
    got = send_rows(lower, [((0, 0), (1, 0))])
    plan = make_plan(pivot_rows.reshape(1, NB))
    lower = jnp.where(zl == 1, after(got, plan), lower)
    got = send_rows(lower, [((a, 0), (a, 1)) for a in (0, 1)])
    sent = pack(jnp.zeros((1,), jnp.int32), after(plan, lower), matrix)
    lower = jnp.where(y == 1, after(got, sent), lower)
    got = send_rows(lower, [((a, s), (a, t)) for a in (0, 1) for s, t in ((0, 3), (1, 2))])
    lower = jnp.where(y >= 2, got, lower)
    rows = lax.all_to_all(after(sent, lower), ROWS, 0, 0)
    rest = later_rounds(after(plan, sent), matrix)
    first, second, half = weigh(lower, panel)

    zs, xs = range(N_ZH), range(N_X)
    quarter = matrix.shape[0] // N_PART
    got = send_cols(half, [((0, 0, 0), (0, 0, 1))])
    first = jnp.where(c == 0, first, got[:quarter])
    second = jnp.where(c == 0, second, got[quarter:])
    got = send_cols(second, [((0, 0, 0), (0, 1, 0)), ((0, 0, 1), (0, 3, 1))])
    piece = jnp.where(x == jnp.where(c == 0, 1, 3), got, first)
    got = send_cols(
        piece,
        [((0, s, 0), (0, t, 0)) for s, t in ((0, 3), (1, 2))]
        + [((0, s, 1), (0, t, 1)) for s, t in ((0, 1), (3, 2))],
    )
    piece = jnp.where((x == 2) | (x == jnp.where(c == 0, 3, 1)), got, piece)
    got = send_cols(
        piece,
        [((0, a, 0), (1, a, 0)) for a in xs] + [((0, a, 1), (3, a, 1)) for a in xs],
    )
    piece = jnp.where(zh == jnp.where(c == 0, 1, 3), got, piece)
    base, factors = prepare(plan, after(rows, piece), rest, matrix)
    got = send_cols(
        piece,
        [((s, a, 0), (t, a, 0)) for a in xs for s, t in ((0, 3), (1, 2))]
        + [((s, a, 1), (t, a, 1)) for a in xs for s, t in ((0, 1), (3, 2))],
    )
    got = after(got, factors)
    piece = jnp.where((zh == 2) | (zh == jnp.where(c == 0, 3, 1)), got, piece)
    chips = [(b, a) for a in xs for b in zs]
    other = send_cols(piece, [((b, a, d), (b, a, 1 - d)) for b, a in chips for d in (0, 1)])
    across = send_cols(
        piece,
        [((b, a, 0), (b, NEAR[a], 0)) for b, a in chips]
        + [((b, a, 1), (b, FAR[a], 1)) for b, a in chips],
    )
    crossed = send_cols(
        piece,
        [((b, a, 0), (b, NEAR[a], 1)) for b, a in chips]
        + [((b, a, 1), (b, FAR[a], 0)) for b, a in chips],
    )
    out = update(0, piece, other, factors, base, None)
    across, crossed, out = lax.optimization_barrier((across, crossed, out))
    return update(1, across, crossed, factors, base, out)


def solution(mesh):
    fine = Mesh(mesh.devices.reshape(2, N_Y, N_ZH, N_X, N_C), ROWS + COLS)
    placed = (P(ROWS, COLS), P())
    return jax.shard_map(
        local, mesh=fine, in_specs=placed, out_specs=P(ROWS, COLS), check_vma=False
    )
```

```python
import functools

import jax
import jax.numpy as jnp
from jax import lax
from jax.experimental import pallas as pl
from jax.experimental.pallas import tpu as pltpu
from jax.sharding import Mesh, PartitionSpec as P

NB = 128
EXACT = lax.Precision.HIGHEST
ROWS = ("zl", "y")
COLS = ("zh", "x", "c")
N_Y, N_X, N_ZH, N_C = 4, 4, 4, 2
N_PROW, N_PCOL = 8, 32
N_PART = 4
STEP = NB // N_PROW
SLOTS = 32
BLOCK = 16
PLAN_ROWS = 8

VMEM = pl.BlockSpec(memory_space=pltpu.VMEM)
SMEM = pl.BlockSpec(memory_space=pltpu.SMEM)
ANY = pl.BlockSpec(memory_space=pl.ANY)


SMALL = pltpu.CompilerParams(vmem_limit_bytes=12 << 20)
LARGE = pltpu.CompilerParams(vmem_limit_bytes=56 << 20)


def prow_id(zl, y):
    return zl * N_Y + y


def pcol_id(zh, x, c):
    return (zh * N_X + x) * N_C + c


def my_place():
    row = prow_id(lax.axis_index("zl"), lax.axis_index("y"))
    col = pcol_id(*(lax.axis_index(name) for name in COLS))
    return row, col


NEAR = (1, 0, 3, 2)
FAR = (3, 2, 1, 0)


def send_cols(value, pairs):
    return lax.ppermute(value, COLS, [(pcol_id(*s), pcol_id(*t)) for s, t in pairs])


def send_rows(value, pairs, cols=range(N_PCOL)):
    pairs = [(prow_id(*s) * N_PCOL + q, prow_id(*t) * N_PCOL + q) for s, t in pairs for q in cols]
    return lax.ppermute(value, ROWS + COLS, pairs)


def after(value, first):
    return lax.optimization_barrier((value, first))[0]


def owned_row(pivot, my_row):
    is_owned = ((pivot >> 7) & (N_PROW - 1)) == my_row
    return is_owned, jnp.where(is_owned, ((pivot >> 10) << 7) + (pivot & (NB - 1)), 0)


def to_column(row):
    size = row.shape[1]
    rows = lax.broadcasted_iota(jnp.int32, (size, size), 0)
    cols = lax.broadcasted_iota(jnp.int32, (size, size), 1)
    return jnp.sum(jnp.where(rows == cols, row, 0.0), axis=1, keepdims=True)


def ranks_of(pivots):
    owner = ((pivots >> 7) & (N_PROW - 1)).astype(jnp.float32)
    rows = lax.broadcasted_iota(jnp.int32, (NB, NB), 0)
    cols = lax.broadcasted_iota(jnp.int32, (NB, NB), 1)
    before = (to_column(owner) == owner) & (rows < cols)
    return jnp.sum(jnp.where(before, 1.0, 0.0), axis=0, keepdims=True)


def plan_kernel(pivots, out):
    my_row, _ = my_place()
    ranks = ranks_of(pivots[...])
    owner = (pivots[...] >> 7) & (N_PROW - 1)
    is_owned, row = owned_row(pivots[...], my_row)
    rank = to_column(jnp.where(is_owned, ranks, -1.0))
    wanted = lax.broadcasted_iota(jnp.int32, (NB, NB), 1).astype(jnp.float32)
    rows = jnp.where(rank == wanted, to_column(row.astype(jnp.float32)), 0.0)
    count = jnp.sum(is_owned.astype(jnp.float32), axis=1, keepdims=True)
    most = jnp.max(ranks, axis=1, keepdims=True) + 1.0
    out[...] = jnp.zeros_like(out)
    out[0:1, :] = owner * NB + ranks.astype(jnp.int32)
    out[1:2, :] = jnp.sum(rows, axis=0, keepdims=True).astype(jnp.int32)
    out[2:3, :] = jnp.broadcast_to(count, (1, NB)).astype(jnp.int32)
    out[3:4, :] = jnp.broadcast_to(most, (1, NB)).astype(jnp.int32)


def make_plan(pivots):
    return pl.pallas_call(
        plan_kernel,
        out_shape=jax.ShapeDtypeStruct((PLAN_ROWS, NB), jnp.int32),
        in_specs=[VMEM],
        out_specs=VMEM,
        compiler_params=SMALL,
        cost_estimate=pl.CostEstimate(flops=0, bytes_accessed=3 << 20, transcendentals=0),
        name="plan",
    )(pivots)


def pack_kernel(turn, plan_hbm, matrix, out, plan, held, top, moved, sems, row_sems, out_sems):
    my_row, _ = my_place()
    on_top = my_row == 0
    load = pltpu.make_async_copy(plan_hbm, plan, sems.at[0])
    load_top = pltpu.make_async_copy(matrix.at[pl.ds(0, NB), :], top, sems.at[1])
    load.start()

    @pl.when(on_top)
    def _():
        load_top.start()

    load.wait()
    first = turn[0] * SLOTS
    copies = [
        pltpu.make_async_copy(
            matrix.at[pl.ds(plan[1, first + i], 1), :], held.at[pl.ds(i, 1), :], row_sems.at[i]
        )
        for i in range(SLOTS)
    ]
    for copy in copies:
        copy.start()

    def held_copy(j):
        return pltpu.make_async_copy(held, out.at[j, pl.ds(0, SLOTS), :], out_sems.at[j])

    def moved_copy(j):
        return pltpu.make_async_copy(
            moved.at[pl.ds(j * SLOTS, SLOTS), :],
            out.at[j, pl.ds(SLOTS, SLOTS), :],
            out_sems.at[N_PROW + j],
        )

    @pl.when(on_top)
    def _():
        load_top.wait()

        def move(j, _):
            for i in range(8):
                entry = plan[0, j * 8 + i]
                rank = entry & (NB - 1)
                place = ((entry >> 7) << 5) + (rank & (SLOTS - 1))
                place = jnp.where((rank >> 5) == turn[0], place, N_PROW * SLOTS)
                moved[pl.ds(place, 1), :] = top[pl.ds(j * 8 + i, 1), :]
            return 0

        lax.fori_loop(0, NB // 8, move, 0)
        for j in range(N_PROW):
            moved_copy(j).start()

    for copy in copies:
        copy.wait()
    for j in range(N_PROW):
        held_copy(j).start()

    @pl.when(on_top)
    def _():
        for j in range(N_PROW):
            moved_copy(j).wait()

    for j in range(N_PROW):
        held_copy(j).wait()


def pack(turn, plan, matrix):
    cols = matrix.shape[1]
    return pl.pallas_call(
        pack_kernel,
        out_shape=jax.ShapeDtypeStruct((N_PROW, 2 * SLOTS, cols), jnp.float32),
        in_specs=[SMEM, ANY, ANY],
        out_specs=ANY,
        scratch_shapes=[
            pltpu.SMEM((PLAN_ROWS, NB), jnp.int32),
            pltpu.VMEM((SLOTS, cols), jnp.float32),
            pltpu.VMEM((NB, cols), jnp.float32),
            pltpu.VMEM(((N_PROW + 1) * SLOTS, cols), jnp.float32),
            pltpu.SemaphoreType.DMA((2,)),
            pltpu.SemaphoreType.DMA((SLOTS,)),
            pltpu.SemaphoreType.DMA((2 * N_PROW,)),
        ],
        compiler_params=LARGE,
        cost_estimate=pl.CostEstimate(flops=0, bytes_accessed=6 << 20, transcendentals=0),
        name="pack",
    )(turn, plan, matrix)


def split(value):
    first = value.astype(jnp.bfloat16)
    rest = value - first.astype(jnp.float32)
    second = rest.astype(jnp.bfloat16)
    third = (rest - second.astype(jnp.float32)).astype(jnp.bfloat16)
    return first, second, third


def exact_dot(a, b):
    a1, a2, a3 = split(a)
    b1, b2, b3 = split(b)
    product = functools.partial(jnp.dot, preferred_element_type=jnp.float32)
    lead = jnp.concatenate([a1, a2], axis=1)
    total = product(jnp.concatenate([a1, a3], axis=1), jnp.concatenate([b3, b1], axis=0))
    total = total + product(lead, jnp.concatenate([b2, b2], axis=0))
    return total + product(lead, jnp.concatenate([b1, b1], axis=0))


def inverse_of(lower):
    rows = lax.broadcasted_iota(jnp.int32, (NB, NB), 0)
    cols = lax.broadcasted_iota(jnp.int32, (NB, NB), 1)
    block_bits = BLOCK.bit_length() - 1
    offset = cols - ((rows >> block_bits) << block_bits)
    lower = jnp.where(rows > cols, lower, 0.0)
    inverse = jnp.where(rows == cols, 1.0, 0.0).reshape(NB // BLOCK, BLOCK, NB)
    for j in range(BLOCK - 1):
        column = jnp.sum(jnp.where(offset == j, lower, 0.0), axis=1, keepdims=True)
        column = column.reshape(NB // BLOCK, BLOCK, 1)
        inverse = inverse - column * inverse[:, j : j + 1, :]
    inverse = inverse.reshape(NB, NB)
    size = BLOCK
    while size < NB:
        shift = size.bit_length()
        same = (rows >> shift) == (cols >> shift)
        below = ((rows & size) != 0) & ((cols & size) == 0)
        part = jnp.where(same & below, lower, 0.0)
        inverse = inverse - exact_dot(inverse, exact_dot(part, inverse))
        size *= 2
    return inverse


def weigh_kernel(block, panel_hbm, *refs):
    quarters, (panel, sem) = refs[:N_PART], refs[N_PART:]
    my_row, my_col = my_place()

    @pl.when(my_col == 0)
    def _():
        copy = pltpu.make_async_copy(panel_hbm, panel, sem)
        copy.start()
        inverse = inverse_of(block[...])
        copy.wait()
        height = quarters[0].shape[0]
        for q, out in enumerate(quarters):
            out[...] = exact_dot(panel[q * height : (q + 1) * height, :], inverse)

        @pl.when(my_row == 0)
        def _():
            quarters[0][:NB, :] = -inverse


def weigh(block, panel):
    height = panel.shape[0]
    quarter = jax.ShapeDtypeStruct((height // N_PART, NB), jnp.float32)
    return pl.pallas_call(
        weigh_kernel,
        out_shape=(quarter,) * N_PART,
        in_specs=[VMEM, ANY],
        out_specs=(VMEM,) * N_PART,
        scratch_shapes=[pltpu.VMEM((height, NB), jnp.float32), pltpu.SemaphoreType.DMA],
        compiler_params=SMALL,
        name="weigh",
    )(block, panel)


def prepare_kernel(plan_hbm, rows, rest, matrix, base, factors, picked, own, plan, sems):
    my_row, my_col = my_place()
    load = pltpu.make_async_copy(plan_hbm, plan, sems.at[0])
    whole = pltpu.make_async_copy(matrix, base, sems.at[1])
    load.start()
    whole.start()
    load.wait()

    def find(j, _):
        for i in range(8):
            k = j * 8 + i
            entry = plan[0, k]
            place = entry & (SLOTS - 1)
            picked[pl.ds(k, 1), :] = rows[entry >> 7, pl.ds(place, 1), :]
        return 0

    lax.fori_loop(0, NB // 8, find, 0)

    def fetch(turn, source, place, target):
        copy = pltpu.make_async_copy(
            rest.at[turn - 1, source, pl.ds(place, 1), :], target, sems.at[0]
        )
        copy.start()
        copy.wait()

    @pl.when(plan[3, 0] > SLOTS)
    def _():
        def find_late(k, _):
            entry = plan[0, k]
            rank = entry & (NB - 1)

            @pl.when(rank >= SLOTS)
            def _():
                fetch(rank >> 5, entry >> 7, rank & (SLOTS - 1), picked.at[pl.ds(k, 1), :])

            return 0

        lax.fori_loop(0, NB, find_late, 0)

    first, second, third = split(picked[...])
    factors[0, :NB, :] = first
    factors[0, NB:, :] = first
    factors[1, :NB, :] = second
    factors[1, NB:, :] = second
    factors[2, :NB, :] = third
    factors[2, NB:, :] = first
    whole.wait()

    @pl.when(my_col == 0)
    def _():
        own[...] = base[:, :NB]

    def swap(i, _):
        base[pl.ds(plan[1, i], 1), :] = rows[0, pl.ds(SLOTS + i, 1), :]
        return 0

    lax.fori_loop(0, jnp.minimum(plan[2, 0], SLOTS), swap, 0)

    def swap_late(i, _):
        place = SLOTS + (i & (SLOTS - 1))
        fetch(i >> 5, 0, place, base.at[pl.ds(plan[1, i], 1), :])
        return 0

    lax.fori_loop(SLOTS, jnp.maximum(plan[2, 0], SLOTS), swap_late, 0)

    @pl.when(my_row == 0)
    def _():
        base[:NB, :] = jnp.zeros((NB, base.shape[1]), jnp.float32)

    @pl.when(my_col == 0)
    def _():
        base[:, :NB] = own[...]
        factors[:, :, :NB] = jnp.zeros((3, 2 * NB, NB), jnp.bfloat16)


def prepare(plan, rows, rest, matrix):
    height, cols = matrix.shape
    return pl.pallas_call(
        prepare_kernel,
        out_shape=(
            jax.ShapeDtypeStruct(matrix.shape, jnp.float32),
            jax.ShapeDtypeStruct((3, 2 * NB, cols), jnp.bfloat16),
        ),
        in_specs=[ANY, VMEM, ANY, ANY],
        out_specs=(VMEM, VMEM),
        scratch_shapes=[
            pltpu.VMEM((NB, cols), jnp.float32),
            pltpu.VMEM((height, NB), jnp.float32),
            pltpu.SMEM((PLAN_ROWS, NB), jnp.int32),
            pltpu.SemaphoreType.DMA((2,)),
        ],
        compiler_params=SMALL,
        cost_estimate=pl.CostEstimate(flops=0, bytes_accessed=9 << 20, transcendentals=0),
        name="prepare",
    )(plan, rows, rest, matrix)


def holdings():
    x, c = lax.axis_index("x"), lax.axis_index("c")
    bits = ((x == 1) | (x == 2)).astype(jnp.int32), (x >= 2).astype(jnp.int32)
    mine = jnp.where(c == 0, bits[0], bits[1])
    other = jnp.where(c == 0, bits[1], bits[0])
    return c, mine, other


def update_kernel(mine, late, piece, factors, base, *refs):
    out, buffer, sem = refs[-3:]
    core, my_bit, other_bit = holdings()
    height = piece.shape[0]
    quarter = 2 * core + (my_bit ^ late) if mine else 2 * (1 - core) + (other_bit ^ late)
    start = pl.multiple_of(quarter * height, height)
    first, second, third = split(piece[...])
    lead = jnp.concatenate([first, second], axis=1)
    tail = jnp.concatenate([first, third], axis=1)
    product = functools.partial(jnp.dot, preferred_element_type=jnp.float32)
    total = product(tail, factors[2]) + product(lead, factors[1]) + product(lead, factors[0])
    buffer[...] = base[pl.ds(start, height), :] - total
    copy = pltpu.make_async_copy(buffer, out.at[pl.ds(start, height), :], sem)
    copy.start()
    copy.wait()


def update(mine, late, piece, factors, base, done):
    height, cols = piece.shape[0], base.shape[1]
    extra = [] if done is None else [done]
    return pl.pallas_call(
        functools.partial(update_kernel, mine, late),
        out_shape=jax.ShapeDtypeStruct(base.shape, jnp.float32),
        in_specs=[VMEM] * 3 + [ANY] * len(extra),
        out_specs=ANY,
        scratch_shapes=[pltpu.VMEM((height, cols), jnp.float32), pltpu.SemaphoreType.DMA],
        input_output_aliases={3: 0} if extra else {},
        compiler_params=SMALL,
        cost_estimate=pl.CostEstimate(flops=0, bytes_accessed=2 << 20, transcendentals=0),
        name="update",
    )(piece, factors, base, *extra)


def blank_kernel(out):
    pass


def blank(shape):
    return pl.pallas_call(
        blank_kernel,
        out_shape=jax.ShapeDtypeStruct(shape, jnp.float32),
        out_specs=ANY,
        compiler_params=SMALL,
        name="blank",
    )()


def later_rounds(plan, matrix):
    most = plan[3, 0]

    def body(state):
        turn, rest = state
        sent = pack(turn.reshape(1), plan, matrix)
        got = lax.all_to_all(sent, ROWS, 0, 0)
        return turn + 1, lax.dynamic_update_slice(rest, got[None], (turn - 1, 0, 0, 0))

    rest = blank((NB // SLOTS - 1, N_PROW, 2 * SLOTS, matrix.shape[1]))
    return lax.while_loop(lambda state: state[0] * SLOTS < most, body, (jnp.int32(1), rest))[1]


def local(matrix, pivot_rows):
    zh, x, c = (lax.axis_index(name) for name in COLS)
    zl, y = (lax.axis_index(name) for name in ROWS)
    panel = lax.optimization_barrier(matrix[:, :NB])
    lower = panel[:NB]
    targets = ((1, 0), (0, 1), (0, 3))
    received = [send_rows(lower, [((0, 0), t)]) for t in targets]
    plan = make_plan(pivot_rows.reshape(1, NB))
    sent = pack(jnp.zeros((1,), jnp.int32), plan, matrix)
    *received, sent = lax.optimization_barrier((*received, sent))
    for (a, b), got in zip(targets, received):
        lower = jnp.where((zl == a) & (y == b), got, lower)
    got = send_rows(
        lower, [((0, 0), (0, 2)), ((1, 0), (1, 2)), ((0, 1), (1, 1)), ((0, 3), (1, 3))]
    )
    lower = jnp.where((y == 2) | ((zl == 1) & (y != 0)), got, lower)
    rows = lax.all_to_all(after(sent, lower), ROWS, 0, 0)
    rest = later_rounds(after(plan, sent), matrix)
    quarters = weigh(lower, panel)

    zs, xs = range(N_ZH), range(N_X)
    to_near = send_cols(quarters[1], [((0, 0, 0), (0, 1, 0))])
    to_far = send_cols(quarters[3], [((0, 0, 0), (0, 3, 1))])
    to_core = send_cols(quarters[2], [((0, 0, 0), (0, 0, 1))])
    piece = jnp.where(
        c == 0, jnp.where(x == 1, to_near, quarters[0]), jnp.where(x == 3, to_far, to_core)
    )
    got = send_cols(
        piece,
        [((0, s, 0), (0, t, 0)) for s, t in ((0, 3), (1, 2))]
        + [((0, s, 1), (0, t, 1)) for s, t in ((0, 1), (3, 2))],
    )
    piece = jnp.where((x == 2) | (x == jnp.where(c == 0, 3, 1)), got, piece)
    got = send_cols(
        piece,
        [((0, a, 0), (1, a, 0)) for a in xs] + [((0, a, 1), (3, a, 1)) for a in xs],
    )
    piece = jnp.where(zh == jnp.where(c == 0, 1, 3), got, piece)
    base, factors = prepare(plan, after(rows, piece), rest, matrix)
    got = send_cols(
        piece,
        [((s, a, 0), (t, a, 0)) for a in xs for s, t in ((0, 3), (1, 2))]
        + [((s, a, 1), (t, a, 1)) for a in xs for s, t in ((0, 1), (3, 2))],
    )
    got = after(got, factors)
    piece = jnp.where((zh == 2) | (zh == jnp.where(c == 0, 3, 1)), got, piece)
    chips = [(b, a) for a in xs for b in zs]
    swap = [((b, a, d), (b, a, 1 - d)) for b, a in chips for d in (0, 1)]
    across = send_cols(
        piece,
        [((b, a, 0), (b, NEAR[a], 0)) for b, a in chips]
        + [((b, a, 1), (b, FAR[a], 1)) for b, a in chips],
    )
    other = send_cols(piece, swap)
    out = update(True, 0, piece, factors, base, None)
    out = update(False, 0, other, factors, base, out)
    across, out = lax.optimization_barrier((across, out))
    other_across = send_cols(across, swap)
    out = update(True, 1, across, factors, base, out)
    return update(False, 1, other_across, factors, base, out)


def solution(mesh):
    fine = Mesh(mesh.devices.reshape(2, N_Y, N_ZH, N_X, N_C), ROWS + COLS)
    placed = (P(ROWS, COLS), P())
    return jax.shard_map(
        local, mesh=fine, in_specs=placed, out_specs=P(ROWS, COLS), check_vma=False
    )
```

```python
import functools

import jax
import jax.numpy as jnp
from jax import lax
from jax.experimental import pallas as pl
from jax.experimental.pallas import tpu as pltpu
from jax.sharding import Mesh, PartitionSpec as P

NB = 128
EXACT = lax.Precision.HIGHEST
ROWS = ("zl", "y")
COLS = ("zh", "x", "c")
N_Y, N_X, N_ZH, N_C = 4, 4, 4, 2
N_PROW, N_PCOL = 8, 32
N_PART = 4
STEP = NB // N_PROW
SLOTS = 32
BLOCK = 16
PLAN_ROWS = 8

VMEM = pl.BlockSpec(memory_space=pltpu.VMEM)
SMEM = pl.BlockSpec(memory_space=pltpu.SMEM)
ANY = pl.BlockSpec(memory_space=pl.ANY)


SMALL = pltpu.CompilerParams(vmem_limit_bytes=12 << 20)
LARGE = pltpu.CompilerParams(vmem_limit_bytes=56 << 20)


def prow_id(zl, y):
    return zl * N_Y + y


def pcol_id(zh, x, c):
    return (zh * N_X + x) * N_C + c


def my_place():
    row = prow_id(lax.axis_index("zl"), lax.axis_index("y"))
    col = pcol_id(*(lax.axis_index(name) for name in COLS))
    return row, col


NEAR = (1, 0, 3, 2)
FAR = (3, 2, 1, 0)


def send_cols(value, pairs):
    return lax.ppermute(value, COLS, [(pcol_id(*s), pcol_id(*t)) for s, t in pairs])


def send_rows(value, pairs, cols=range(N_PCOL)):
    pairs = [(prow_id(*s) * N_PCOL + q, prow_id(*t) * N_PCOL + q) for s, t in pairs for q in cols]
    return lax.ppermute(value, ROWS + COLS, pairs)


def send_along_zh(value, routes):
    pairs = []
    for zl in range(2):
        for y in range(N_Y):
            for a in range(N_X):
                for d in range(N_C):
                    for s, t in routes[zl ^ d]:
                        row = prow_id(zl, y) * N_PCOL
                        pairs.append((row + pcol_id(s, a, d), row + pcol_id(t, a, d)))
    return lax.ppermute(value, ROWS + COLS, pairs)


def after(value, first):
    return lax.optimization_barrier((value, first))[0]


def owned_row(pivot, my_row):
    is_owned = ((pivot >> 7) & (N_PROW - 1)) == my_row
    return is_owned, jnp.where(is_owned, ((pivot >> 10) << 7) + (pivot & (NB - 1)), 0)


def to_column(row):
    size = row.shape[1]
    rows = lax.broadcasted_iota(jnp.int32, (size, size), 0)
    cols = lax.broadcasted_iota(jnp.int32, (size, size), 1)
    return jnp.sum(jnp.where(rows == cols, row, 0.0), axis=1, keepdims=True)


def ranks_of(pivots):
    owner = ((pivots >> 7) & (N_PROW - 1)).astype(jnp.float32)
    rows = lax.broadcasted_iota(jnp.int32, (NB, NB), 0)
    cols = lax.broadcasted_iota(jnp.int32, (NB, NB), 1)
    before = (to_column(owner) == owner) & (rows < cols)
    return jnp.sum(jnp.where(before, 1.0, 0.0), axis=0, keepdims=True)


def plan_kernel(pivots, out):
    my_row, _ = my_place()
    ranks = ranks_of(pivots[...])
    owner = (pivots[...] >> 7) & (N_PROW - 1)
    is_owned, row = owned_row(pivots[...], my_row)
    rank = to_column(jnp.where(is_owned, ranks, -1.0))
    wanted = lax.broadcasted_iota(jnp.int32, (NB, NB), 1).astype(jnp.float32)
    rows = jnp.where(rank == wanted, to_column(row.astype(jnp.float32)), 0.0)
    count = jnp.sum(is_owned.astype(jnp.float32), axis=1, keepdims=True)
    most = jnp.max(ranks, axis=1, keepdims=True) + 1.0
    out[...] = jnp.zeros_like(out)
    out[0:1, :] = owner * NB + ranks.astype(jnp.int32)
    out[1:2, :] = jnp.sum(rows, axis=0, keepdims=True).astype(jnp.int32)
    out[2:3, :] = jnp.broadcast_to(count, (1, NB)).astype(jnp.int32)
    out[3:4, :] = jnp.broadcast_to(most, (1, NB)).astype(jnp.int32)


def make_plan(pivots):
    return pl.pallas_call(
        plan_kernel,
        out_shape=jax.ShapeDtypeStruct((PLAN_ROWS, NB), jnp.int32),
        in_specs=[VMEM],
        out_specs=VMEM,
        compiler_params=SMALL,
        cost_estimate=pl.CostEstimate(flops=0, bytes_accessed=3 << 20, transcendentals=0),
        name="plan",
    )(pivots)


def pack_kernel(turn, plan_hbm, matrix, out, plan, held, top, moved, sems, row_sems, out_sems):
    my_row, _ = my_place()
    on_top = my_row == 0
    load = pltpu.make_async_copy(plan_hbm, plan, sems.at[0])
    load_top = pltpu.make_async_copy(matrix.at[pl.ds(0, NB), :], top, sems.at[1])
    load.start()

    @pl.when(on_top)
    def _():
        load_top.start()

    load.wait()
    first = turn[0] * SLOTS
    copies = [
        pltpu.make_async_copy(
            matrix.at[pl.ds(plan[1, first + i], 1), :], held.at[pl.ds(i, 1), :], row_sems.at[i]
        )
        for i in range(SLOTS)
    ]
    for copy in copies:
        copy.start()

    def held_copy(j):
        return pltpu.make_async_copy(held, out.at[j, pl.ds(0, SLOTS), :], out_sems.at[j])

    def moved_copy(j):
        return pltpu.make_async_copy(
            moved.at[pl.ds(j * SLOTS, SLOTS), :],
            out.at[j, pl.ds(SLOTS, SLOTS), :],
            out_sems.at[N_PROW + j],
        )

    @pl.when(on_top)
    def _():
        load_top.wait()

        def move(j, _):
            for i in range(8):
                entry = plan[0, j * 8 + i]
                rank = entry & (NB - 1)
                place = ((entry >> 7) << 5) + (rank & (SLOTS - 1))
                place = jnp.where((rank >> 5) == turn[0], place, N_PROW * SLOTS)
                moved[pl.ds(place, 1), :] = top[pl.ds(j * 8 + i, 1), :]
            return 0

        lax.fori_loop(0, NB // 8, move, 0)
        for j in range(N_PROW):
            moved_copy(j).start()

    for copy in copies:
        copy.wait()
    for j in range(N_PROW):
        held_copy(j).start()

    @pl.when(on_top)
    def _():
        for j in range(N_PROW):
            moved_copy(j).wait()

    for j in range(N_PROW):
        held_copy(j).wait()


def pack(turn, plan, matrix):
    cols = matrix.shape[1]
    return pl.pallas_call(
        pack_kernel,
        out_shape=jax.ShapeDtypeStruct((N_PROW, 2 * SLOTS, cols), jnp.float32),
        in_specs=[SMEM, ANY, ANY],
        out_specs=ANY,
        scratch_shapes=[
            pltpu.SMEM((PLAN_ROWS, NB), jnp.int32),
            pltpu.VMEM((SLOTS, cols), jnp.float32),
            pltpu.VMEM((NB, cols), jnp.float32),
            pltpu.VMEM(((N_PROW + 1) * SLOTS, cols), jnp.float32),
            pltpu.SemaphoreType.DMA((2,)),
            pltpu.SemaphoreType.DMA((SLOTS,)),
            pltpu.SemaphoreType.DMA((2 * N_PROW,)),
        ],
        compiler_params=LARGE,
        cost_estimate=pl.CostEstimate(flops=0, bytes_accessed=6 << 20, transcendentals=0),
        name="pack",
    )(turn, plan, matrix)


def split(value):
    first = value.astype(jnp.bfloat16)
    rest = value - first.astype(jnp.float32)
    second = rest.astype(jnp.bfloat16)
    third = (rest - second.astype(jnp.float32)).astype(jnp.bfloat16)
    return first, second, third


def exact_dot(a, b):
    a1, a2, a3 = split(a)
    b1, b2, b3 = split(b)
    product = functools.partial(jnp.dot, preferred_element_type=jnp.float32)
    lead = jnp.concatenate([a1, a2], axis=1)
    total = product(jnp.concatenate([a1, a3], axis=1), jnp.concatenate([b3, b1], axis=0))
    total = total + product(lead, jnp.concatenate([b2, b2], axis=0))
    return total + product(lead, jnp.concatenate([b1, b1], axis=0))


def inverse_of(lower):
    rows = lax.broadcasted_iota(jnp.int32, (NB, NB), 0)
    cols = lax.broadcasted_iota(jnp.int32, (NB, NB), 1)
    block_bits = BLOCK.bit_length() - 1
    offset = cols - ((rows >> block_bits) << block_bits)
    lower = jnp.where(rows > cols, lower, 0.0)
    inverse = jnp.where(rows == cols, 1.0, 0.0).reshape(NB // BLOCK, BLOCK, NB)
    for j in range(BLOCK - 1):
        column = jnp.sum(jnp.where(offset == j, lower, 0.0), axis=1, keepdims=True)
        column = column.reshape(NB // BLOCK, BLOCK, 1)
        inverse = inverse - column * inverse[:, j : j + 1, :]
    inverse = inverse.reshape(NB, NB)
    size = BLOCK
    while size < NB:
        shift = size.bit_length()
        same = (rows >> shift) == (cols >> shift)
        below = ((rows & size) != 0) & ((cols & size) == 0)
        part = jnp.where(same & below, lower, 0.0)
        inverse = inverse - exact_dot(inverse, exact_dot(part, inverse))
        size *= 2
    return inverse


def weigh_kernel(block, panel_hbm, *refs):
    quarters, (panel, sem) = refs[:N_PART], refs[N_PART:]
    my_row, my_col = my_place()

    @pl.when(my_col == 0)
    def _():
        copy = pltpu.make_async_copy(panel_hbm, panel, sem)
        copy.start()
        inverse = inverse_of(block[...])
        copy.wait()
        height = quarters[0].shape[0]
        for q, out in enumerate(quarters):
            out[...] = exact_dot(panel[q * height : (q + 1) * height, :], inverse)

        @pl.when(my_row == 0)
        def _():
            quarters[0][:NB, :] = -inverse


def weigh(block, panel):
    height = panel.shape[0]
    quarter = jax.ShapeDtypeStruct((height // N_PART, NB), jnp.float32)
    return pl.pallas_call(
        weigh_kernel,
        out_shape=(quarter,) * N_PART,
        in_specs=[VMEM, ANY],
        out_specs=(VMEM,) * N_PART,
        scratch_shapes=[pltpu.VMEM((height, NB), jnp.float32), pltpu.SemaphoreType.DMA],
        compiler_params=SMALL,
        name="weigh",
    )(block, panel)


def prepare_kernel(plan_hbm, rows, rest, matrix, base, factors, picked, own, plan, sems):
    my_row, my_col = my_place()
    load = pltpu.make_async_copy(plan_hbm, plan, sems.at[0])
    whole = pltpu.make_async_copy(matrix, base, sems.at[1])
    load.start()
    whole.start()
    load.wait()

    def find(j, _):
        for i in range(8):
            k = j * 8 + i
            entry = plan[0, k]
            place = entry & (SLOTS - 1)
            picked[pl.ds(k, 1), :] = rows[entry >> 7, pl.ds(place, 1), :]
        return 0

    lax.fori_loop(0, NB // 8, find, 0)

    def fetch(turn, source, place, target):
        copy = pltpu.make_async_copy(
            rest.at[turn - 1, source, pl.ds(place, 1), :], target, sems.at[0]
        )
        copy.start()
        copy.wait()

    @pl.when(plan[3, 0] > SLOTS)
    def _():
        def find_late(k, _):
            entry = plan[0, k]
            rank = entry & (NB - 1)

            @pl.when(rank >= SLOTS)
            def _():
                fetch(rank >> 5, entry >> 7, rank & (SLOTS - 1), picked.at[pl.ds(k, 1), :])

            return 0

        lax.fori_loop(0, NB, find_late, 0)

    first, second, third = split(picked[...])
    factors[0, :NB, :] = first
    factors[0, NB:, :] = first
    factors[1, :NB, :] = second
    factors[1, NB:, :] = second
    factors[2, :NB, :] = third
    factors[2, NB:, :] = first
    whole.wait()

    @pl.when(my_col == 0)
    def _():
        own[...] = base[:, :NB]

    def swap(i, _):
        base[pl.ds(plan[1, i], 1), :] = rows[0, pl.ds(SLOTS + i, 1), :]
        return 0

    lax.fori_loop(0, jnp.minimum(plan[2, 0], SLOTS), swap, 0)

    def swap_late(i, _):
        place = SLOTS + (i & (SLOTS - 1))
        fetch(i >> 5, 0, place, base.at[pl.ds(plan[1, i], 1), :])
        return 0

    lax.fori_loop(SLOTS, jnp.maximum(plan[2, 0], SLOTS), swap_late, 0)

    @pl.when(my_row == 0)
    def _():
        base[:NB, :] = jnp.zeros((NB, base.shape[1]), jnp.float32)

    @pl.when(my_col == 0)
    def _():
        base[:, :NB] = own[...]
        factors[:, :, :NB] = jnp.zeros((3, 2 * NB, NB), jnp.bfloat16)


def prepare(plan, rows, rest, matrix):
    height, cols = matrix.shape
    return pl.pallas_call(
        prepare_kernel,
        out_shape=(
            jax.ShapeDtypeStruct(matrix.shape, jnp.float32),
            jax.ShapeDtypeStruct((3, 2 * NB, cols), jnp.bfloat16),
        ),
        in_specs=[ANY, VMEM, ANY, ANY],
        out_specs=(VMEM, VMEM),
        scratch_shapes=[
            pltpu.VMEM((NB, cols), jnp.float32),
            pltpu.VMEM((height, NB), jnp.float32),
            pltpu.SMEM((PLAN_ROWS, NB), jnp.int32),
            pltpu.SemaphoreType.DMA((2,)),
        ],
        compiler_params=SMALL,
        cost_estimate=pl.CostEstimate(flops=0, bytes_accessed=9 << 20, transcendentals=0),
        name="prepare",
    )(plan, rows, rest, matrix)


def holdings():
    x, c = lax.axis_index("x"), lax.axis_index("c")
    bits = ((x == 1) | (x == 2)).astype(jnp.int32), (x >= 2).astype(jnp.int32)
    mine = jnp.where(c == 0, bits[0], bits[1])
    other = jnp.where(c == 0, bits[1], bits[0])
    return c, mine, other


def update_kernel(mine, late, piece, factors, base, *refs):
    out, buffer, sem = refs[-3:]
    core, my_bit, other_bit = holdings()
    height = piece.shape[0]
    quarter = 2 * core + (my_bit ^ late) if mine else 2 * (1 - core) + (other_bit ^ late)
    start = pl.multiple_of(quarter * height, height)
    first, second, third = split(piece[...])
    lead = jnp.concatenate([first, second], axis=1)
    tail = jnp.concatenate([first, third], axis=1)
    product = functools.partial(jnp.dot, preferred_element_type=jnp.float32)
    total = product(tail, factors[2]) + product(lead, factors[1]) + product(lead, factors[0])
    buffer[...] = base[pl.ds(start, height), :] - total
    copy = pltpu.make_async_copy(buffer, out.at[pl.ds(start, height), :], sem)
    copy.start()
    copy.wait()


def update(mine, late, piece, factors, base, done):
    height, cols = piece.shape[0], base.shape[1]
    extra = [] if done is None else [done]
    return pl.pallas_call(
        functools.partial(update_kernel, mine, late),
        out_shape=jax.ShapeDtypeStruct(base.shape, jnp.float32),
        in_specs=[VMEM] * 3 + [ANY] * len(extra),
        out_specs=ANY,
        scratch_shapes=[pltpu.VMEM((height, cols), jnp.float32), pltpu.SemaphoreType.DMA],
        input_output_aliases={3: 0} if extra else {},
        compiler_params=SMALL,
        cost_estimate=pl.CostEstimate(flops=0, bytes_accessed=2 << 20, transcendentals=0),
        name="update",
    )(piece, factors, base, *extra)


def blank_kernel(out):
    pass


def blank(shape):
    return pl.pallas_call(
        blank_kernel,
        out_shape=jax.ShapeDtypeStruct(shape, jnp.float32),
        out_specs=ANY,
        compiler_params=SMALL,
        name="blank",
    )()


def later_rounds(plan, matrix):
    most = plan[3, 0]

    def body(state):
        turn, rest = state
        sent = pack(turn.reshape(1), plan, matrix)
        got = lax.all_to_all(sent, ROWS, 0, 0)
        return turn + 1, lax.dynamic_update_slice(rest, got[None], (turn - 1, 0, 0, 0))

    rest = blank((NB // SLOTS - 1, N_PROW, 2 * SLOTS, matrix.shape[1]))
    return lax.while_loop(lambda state: state[0] * SLOTS < most, body, (jnp.int32(1), rest))[1]


def local(matrix, pivot_rows):
    zh, x, c = (lax.axis_index(name) for name in COLS)
    zl, y = (lax.axis_index(name) for name in ROWS)
    panel = lax.optimization_barrier(matrix[:, :NB])
    lower = panel[:NB]
    targets = ((1, 0), (0, 1), (0, 3))
    received = [send_rows(lower, [((0, 0), t)], [0]) for t in targets]
    plan = make_plan(pivot_rows.reshape(1, NB))
    *received, plan = lax.optimization_barrier((*received, plan))
    for (a, b), got in zip(targets, received):
        lower = jnp.where((zl == a) & (y == b), got, lower)
    got = send_rows(
        lower, [((0, 0), (0, 2)), ((1, 0), (1, 2)), ((0, 1), (1, 1)), ((0, 3), (1, 3))], [0]
    )
    sent = pack(jnp.zeros((1,), jnp.int32), after(plan, lower), matrix)
    got, sent = lax.optimization_barrier((got, sent))
    lower = jnp.where((y == 2) | ((zl == 1) & (y != 0)), got, lower)
    rows = lax.all_to_all(after(sent, lower), ROWS, 0, 0)
    rest = later_rounds(after(plan, sent), matrix)
    quarters = weigh(lower, panel)

    zs, xs = range(N_ZH), range(N_X)
    to_near = send_cols(quarters[1], [((0, 0, 0), (0, 1, 0))])
    to_far = send_cols(quarters[3], [((0, 0, 0), (0, 3, 1))])
    to_core = send_cols(quarters[2], [((0, 0, 0), (0, 0, 1))])
    piece = jnp.where(
        c == 0, jnp.where(x == 1, to_near, quarters[0]), jnp.where(x == 3, to_far, to_core)
    )
    got = send_cols(
        piece,
        [((0, s, 0), (0, t, 0)) for s, t in ((0, 3), (1, 2))]
        + [((0, s, 1), (0, t, 1)) for s, t in ((0, 1), (3, 2))],
    )
    piece = jnp.where((x == 2) | (x == jnp.where(c == 0, 3, 1)), got, piece)
    upward = (c ^ zl) == 0
    got = send_along_zh(piece, (((0, 1),), ((0, 3),)))
    piece = jnp.where(zh == jnp.where(upward, 1, 3), got, piece)
    base, factors = prepare(plan, after(rows, piece), rest, matrix)
    got = send_along_zh(piece, (((0, 3), (1, 2)), ((0, 1), (3, 2))))
    got = after(got, factors)
    piece = jnp.where((zh == 2) | (zh == jnp.where(upward, 3, 1)), got, piece)
    chips = [(b, a) for a in xs for b in zs]
    swap = [((b, a, d), (b, a, 1 - d)) for b, a in chips for d in (0, 1)]
    across = send_cols(
        piece,
        [((b, a, 0), (b, NEAR[a], 0)) for b, a in chips]
        + [((b, a, 1), (b, FAR[a], 1)) for b, a in chips],
    )
    other = send_cols(piece, swap)
    out = update(True, 0, piece, factors, base, None)
    out = update(False, 0, other, factors, base, out)
    across, out = lax.optimization_barrier((across, out))
    other_across = send_cols(across, swap)
    out = update(True, 1, across, factors, base, out)
    return update(False, 1, other_across, factors, base, out)


def solution(mesh):
    fine = Mesh(mesh.devices.reshape(2, N_Y, N_ZH, N_X, N_C), ROWS + COLS)
    placed = (P(ROWS, COLS), P())
    return jax.shard_map(
        local, mesh=fine, in_specs=placed, out_specs=P(ROWS, COLS), check_vma=False
    )
```

```python
import functools

import jax
import jax.numpy as jnp
from jax import lax
from jax.experimental import pallas as pl
from jax.experimental.pallas import tpu as pltpu
from jax.sharding import Mesh, PartitionSpec as P

NB = 128
EXACT = lax.Precision.HIGHEST
ROWS = ("zl", "y")
COLS = ("zh", "x", "c")
N_Y, N_X, N_ZH, N_C = 4, 4, 4, 2
N_PROW, N_PCOL = 8, 32
N_PART = 4
STEP = NB // N_PROW
SLOTS = 32
BLOCK = 32
PLAN_ROWS = 8

VMEM = pl.BlockSpec(memory_space=pltpu.VMEM)
SMEM = pl.BlockSpec(memory_space=pltpu.SMEM)
ANY = pl.BlockSpec(memory_space=pl.ANY)


SMALL = pltpu.CompilerParams(vmem_limit_bytes=12 << 20)
LARGE = pltpu.CompilerParams(vmem_limit_bytes=56 << 20)


def prow_id(zl, y):
    return zl * N_Y + y


def pcol_id(zh, x, c):
    return (zh * N_X + x) * N_C + c


def my_place():
    row = prow_id(lax.axis_index("zl"), lax.axis_index("y"))
    col = pcol_id(*(lax.axis_index(name) for name in COLS))
    return row, col


NEAR = (1, 0, 3, 2)
FAR = (3, 2, 1, 0)


def send_cols(value, pairs):
    return lax.ppermute(value, COLS, [(pcol_id(*s), pcol_id(*t)) for s, t in pairs])


def send_rows(value, pairs, cols=range(N_PCOL)):
    pairs = [(prow_id(*s) * N_PCOL + q, prow_id(*t) * N_PCOL + q) for s, t in pairs for q in cols]
    return lax.ppermute(value, ROWS + COLS, pairs)


def send_along_zh(value, routes):
    pairs = []
    for zl in range(2):
        for y in range(N_Y):
            for a in range(N_X):
                for d in range(N_C):
                    for s, t in routes[zl ^ d]:
                        row = prow_id(zl, y) * N_PCOL
                        pairs.append((row + pcol_id(s, a, d), row + pcol_id(t, a, d)))
    return lax.ppermute(value, ROWS + COLS, pairs)


def after(value, first):
    return lax.optimization_barrier((value, first))[0]


def owned_row(pivot, my_row):
    is_owned = ((pivot >> 7) & (N_PROW - 1)) == my_row
    return is_owned, jnp.where(is_owned, ((pivot >> 10) << 7) + (pivot & (NB - 1)), 0)


def to_column(row):
    size = row.shape[1]
    rows = lax.broadcasted_iota(jnp.int32, (size, size), 0)
    cols = lax.broadcasted_iota(jnp.int32, (size, size), 1)
    return jnp.sum(jnp.where(rows == cols, row, 0.0), axis=1, keepdims=True)


def ranks_of(pivots):
    owner = ((pivots >> 7) & (N_PROW - 1)).astype(jnp.float32)
    rows = lax.broadcasted_iota(jnp.int32, (NB, NB), 0)
    cols = lax.broadcasted_iota(jnp.int32, (NB, NB), 1)
    before = (to_column(owner) == owner) & (rows < cols)
    return jnp.sum(jnp.where(before, 1.0, 0.0), axis=0, keepdims=True)


def plan_kernel(pivots, out):
    my_row, _ = my_place()
    ranks = ranks_of(pivots[...])
    owner = (pivots[...] >> 7) & (N_PROW - 1)
    is_owned, row = owned_row(pivots[...], my_row)
    rank = to_column(jnp.where(is_owned, ranks, -1.0))
    wanted = lax.broadcasted_iota(jnp.int32, (NB, NB), 1).astype(jnp.float32)
    rows = jnp.where(rank == wanted, to_column(row.astype(jnp.float32)), 0.0)
    count = jnp.sum(is_owned.astype(jnp.float32), axis=1, keepdims=True)
    most = jnp.max(ranks, axis=1, keepdims=True) + 1.0
    out[...] = jnp.zeros_like(out)
    out[0:1, :] = owner * NB + ranks.astype(jnp.int32)
    out[1:2, :] = jnp.sum(rows, axis=0, keepdims=True).astype(jnp.int32)
    out[2:3, :] = jnp.broadcast_to(count, (1, NB)).astype(jnp.int32)
    out[3:4, :] = jnp.broadcast_to(most, (1, NB)).astype(jnp.int32)


def make_plan(pivots):
    return pl.pallas_call(
        plan_kernel,
        out_shape=jax.ShapeDtypeStruct((PLAN_ROWS, NB), jnp.int32),
        in_specs=[VMEM],
        out_specs=VMEM,
        compiler_params=SMALL,
        cost_estimate=pl.CostEstimate(flops=0, bytes_accessed=3 << 20, transcendentals=0),
        name="plan",
    )(pivots)


def pack_kernel(turn, plan, matrix, out, held, top, moved, sem, row_sems, out_sems):
    my_row, _ = my_place()
    on_top = my_row == 0
    load_top = pltpu.make_async_copy(matrix.at[pl.ds(0, NB), :], top, sem)

    @pl.when(on_top)
    def _():
        load_top.start()

    first = turn[0] * SLOTS
    copies = [
        pltpu.make_async_copy(
            matrix.at[pl.ds(plan[1, first + i], 1), :], held.at[pl.ds(i, 1), :], row_sems.at[i]
        )
        for i in range(SLOTS)
    ]
    for copy in copies:
        copy.start()

    def held_copy(j):
        return pltpu.make_async_copy(held, out.at[j, pl.ds(0, SLOTS), :], out_sems.at[j])

    def moved_copy(j):
        return pltpu.make_async_copy(
            moved.at[pl.ds(j * SLOTS, SLOTS), :],
            out.at[j, pl.ds(SLOTS, SLOTS), :],
            out_sems.at[N_PROW + j],
        )

    @pl.when(on_top)
    def _():
        load_top.wait()

        def move(j, _):
            for i in range(8):
                entry = plan[0, j * 8 + i]
                rank = entry & (NB - 1)
                place = ((entry >> 7) << 5) + (rank & (SLOTS - 1))
                place = jnp.where((rank >> 5) == turn[0], place, N_PROW * SLOTS)
                moved[pl.ds(place, 1), :] = top[pl.ds(j * 8 + i, 1), :]
            return 0

        lax.fori_loop(0, NB // 8, move, 0)
        for j in range(N_PROW):
            moved_copy(j).start()

    for copy in copies:
        copy.wait()
    for j in range(N_PROW):
        held_copy(j).start()

    @pl.when(on_top)
    def _():
        for j in range(N_PROW):
            moved_copy(j).wait()

    for j in range(N_PROW):
        held_copy(j).wait()


def pack(turn, plan, matrix):
    cols = matrix.shape[1]
    return pl.pallas_call(
        pack_kernel,
        out_shape=jax.ShapeDtypeStruct((N_PROW, 2 * SLOTS, cols), jnp.float32),
        in_specs=[SMEM, SMEM, ANY],
        out_specs=ANY,
        scratch_shapes=[
            pltpu.VMEM((SLOTS, cols), jnp.float32),
            pltpu.VMEM((NB, cols), jnp.float32),
            pltpu.VMEM(((N_PROW + 1) * SLOTS, cols), jnp.float32),
            pltpu.SemaphoreType.DMA,
            pltpu.SemaphoreType.DMA((SLOTS,)),
            pltpu.SemaphoreType.DMA((2 * N_PROW,)),
        ],
        compiler_params=LARGE,
        cost_estimate=pl.CostEstimate(flops=0, bytes_accessed=6 << 20, transcendentals=0),
        name="pack",
    )(turn, plan, matrix)


def split(value):
    first = value.astype(jnp.bfloat16)
    rest = value - first.astype(jnp.float32)
    second = rest.astype(jnp.bfloat16)
    third = (rest - second.astype(jnp.float32)).astype(jnp.bfloat16)
    return first, second, third


def exact_dot(a, b):
    a1, a2, a3 = split(a)
    b1, b2, b3 = split(b)
    product = functools.partial(jnp.dot, preferred_element_type=jnp.float32)
    lead = jnp.concatenate([a1, a2], axis=1)
    total = product(jnp.concatenate([a1, a3], axis=1), jnp.concatenate([b3, b1], axis=0))
    total = total + product(lead, jnp.concatenate([b2, b2], axis=0))
    return total + product(lead, jnp.concatenate([b1, b1], axis=0))


def inverse_of(lower):
    rows = lax.broadcasted_iota(jnp.int32, (NB, NB), 0)
    cols = lax.broadcasted_iota(jnp.int32, (NB, NB), 1)
    block_bits = BLOCK.bit_length() - 1
    offset = cols - ((rows >> block_bits) << block_bits)
    lower = jnp.where(rows > cols, lower, 0.0)
    inverse = jnp.where(rows == cols, 1.0, 0.0).reshape(NB // BLOCK, BLOCK, NB)
    for j in range(BLOCK - 1):
        column = jnp.sum(jnp.where(offset == j, lower, 0.0), axis=1, keepdims=True)
        column = column.reshape(NB // BLOCK, BLOCK, 1)
        inverse = inverse - column * inverse[:, j : j + 1, :]
    inverse = inverse.reshape(NB, NB)
    size = BLOCK
    while size < NB:
        shift = size.bit_length()
        same = (rows >> shift) == (cols >> shift)
        below = ((rows & size) != 0) & ((cols & size) == 0)
        part = jnp.where(same & below, lower, 0.0)
        inverse = inverse - exact_dot(inverse, exact_dot(part, inverse))
        size *= 2
    return inverse


def weigh_kernel(block, panel_hbm, *refs):
    quarters, (panel, sem) = refs[:N_PART], refs[N_PART:]
    my_row, my_col = my_place()

    @pl.when(my_col == 0)
    def _():
        copy = pltpu.make_async_copy(panel_hbm, panel, sem)
        copy.start()
        inverse = inverse_of(block[...])
        copy.wait()
        height = quarters[0].shape[0]
        for q, out in enumerate(quarters):
            out[...] = exact_dot(panel[q * height : (q + 1) * height, :], inverse)

        @pl.when(my_row == 0)
        def _():
            quarters[0][:NB, :] = -inverse


def weigh(block, panel):
    height = panel.shape[0]
    quarter = jax.ShapeDtypeStruct((height // N_PART, NB), jnp.float32)
    return pl.pallas_call(
        weigh_kernel,
        out_shape=(quarter,) * N_PART,
        in_specs=[VMEM, ANY],
        out_specs=(VMEM,) * N_PART,
        scratch_shapes=[pltpu.VMEM((height, NB), jnp.float32), pltpu.SemaphoreType.DMA],
        compiler_params=SMALL,
        name="weigh",
    )(block, panel)


def prepare_kernel(plan_hbm, rows, rest, matrix, base, factors, picked, own, plan, sems):
    my_row, my_col = my_place()
    load = pltpu.make_async_copy(plan_hbm, plan, sems.at[0])
    whole = pltpu.make_async_copy(matrix, base, sems.at[1])
    load.start()
    whole.start()
    load.wait()

    def find(j, _):
        for i in range(8):
            k = j * 8 + i
            entry = plan[0, k]
            place = entry & (SLOTS - 1)
            picked[pl.ds(k, 1), :] = rows[entry >> 7, pl.ds(place, 1), :]
        return 0

    lax.fori_loop(0, NB // 8, find, 0)

    def fetch(turn, source, place, target):
        copy = pltpu.make_async_copy(
            rest.at[turn - 1, source, pl.ds(place, 1), :], target, sems.at[0]
        )
        copy.start()
        copy.wait()

    @pl.when(plan[3, 0] > SLOTS)
    def _():
        def find_late(k, _):
            entry = plan[0, k]
            rank = entry & (NB - 1)

            @pl.when(rank >= SLOTS)
            def _():
                fetch(rank >> 5, entry >> 7, rank & (SLOTS - 1), picked.at[pl.ds(k, 1), :])

            return 0

        lax.fori_loop(0, NB, find_late, 0)

    first, second, third = split(picked[...])
    factors[0, :NB, :] = first
    factors[0, NB:, :] = first
    factors[1, :NB, :] = second
    factors[1, NB:, :] = second
    factors[2, :NB, :] = third
    factors[2, NB:, :] = first
    whole.wait()

    @pl.when(my_col == 0)
    def _():
        own[...] = base[:, :NB]

    def swap(i, _):
        base[pl.ds(plan[1, i], 1), :] = rows[0, pl.ds(SLOTS + i, 1), :]
        return 0

    lax.fori_loop(0, jnp.minimum(plan[2, 0], SLOTS), swap, 0)

    def swap_late(i, _):
        place = SLOTS + (i & (SLOTS - 1))
        fetch(i >> 5, 0, place, base.at[pl.ds(plan[1, i], 1), :])
        return 0

    lax.fori_loop(SLOTS, jnp.maximum(plan[2, 0], SLOTS), swap_late, 0)

    @pl.when(my_row == 0)
    def _():
        base[:NB, :] = jnp.zeros((NB, base.shape[1]), jnp.float32)

    @pl.when(my_col == 0)
    def _():
        base[:, :NB] = own[...]
        factors[:, :, :NB] = jnp.zeros((3, 2 * NB, NB), jnp.bfloat16)


def prepare(plan, rows, rest, matrix):
    height, cols = matrix.shape
    return pl.pallas_call(
        prepare_kernel,
        out_shape=(
            jax.ShapeDtypeStruct(matrix.shape, jnp.float32),
            jax.ShapeDtypeStruct((3, 2 * NB, cols), jnp.bfloat16),
        ),
        in_specs=[ANY, VMEM, ANY, ANY],
        out_specs=(VMEM, VMEM),
        scratch_shapes=[
            pltpu.VMEM((NB, cols), jnp.float32),
            pltpu.VMEM((height, NB), jnp.float32),
            pltpu.SMEM((PLAN_ROWS, NB), jnp.int32),
            pltpu.SemaphoreType.DMA((2,)),
        ],
        compiler_params=SMALL,
        cost_estimate=pl.CostEstimate(flops=0, bytes_accessed=9 << 20, transcendentals=0),
        name="prepare",
    )(plan, rows, rest, matrix)


def holdings():
    x, c = lax.axis_index("x"), lax.axis_index("c")
    bits = ((x == 1) | (x == 2)).astype(jnp.int32), (x >= 2).astype(jnp.int32)
    mine = jnp.where(c == 0, bits[0], bits[1])
    other = jnp.where(c == 0, bits[1], bits[0])
    return c, mine, other


def update_kernel(mine, late, piece, factors, base, *refs):
    out, buffer, sem = refs[-3:]
    core, my_bit, other_bit = holdings()
    height = piece.shape[0]
    quarter = 2 * core + (my_bit ^ late) if mine else 2 * (1 - core) + (other_bit ^ late)
    start = pl.multiple_of(quarter * height, height)
    first, second, third = split(piece[...])
    lead = jnp.concatenate([first, second], axis=1)
    tail = jnp.concatenate([first, third], axis=1)
    product = functools.partial(jnp.dot, preferred_element_type=jnp.float32)
    total = product(tail, factors[2]) + product(lead, factors[1]) + product(lead, factors[0])
    buffer[...] = base[pl.ds(start, height), :] - total
    copy = pltpu.make_async_copy(buffer, out.at[pl.ds(start, height), :], sem)
    copy.start()
    copy.wait()


def update(mine, late, piece, factors, base, done):
    height, cols = piece.shape[0], base.shape[1]
    extra = [] if done is None else [done]
    return pl.pallas_call(
        functools.partial(update_kernel, mine, late),
        out_shape=jax.ShapeDtypeStruct(base.shape, jnp.float32),
        in_specs=[VMEM] * 3 + [ANY] * len(extra),
        out_specs=ANY,
        scratch_shapes=[pltpu.VMEM((height, cols), jnp.float32), pltpu.SemaphoreType.DMA],
        input_output_aliases={3: 0} if extra else {},
        compiler_params=SMALL,
        cost_estimate=pl.CostEstimate(flops=0, bytes_accessed=2 << 20, transcendentals=0),
        name="update",
    )(piece, factors, base, *extra)


def blank_kernel(out):
    pass


def blank(shape):
    return pl.pallas_call(
        blank_kernel,
        out_shape=jax.ShapeDtypeStruct(shape, jnp.float32),
        out_specs=ANY,
        compiler_params=SMALL,
        name="blank",
    )()


def later_rounds(plan, matrix):
    most = plan[3, 0]

    def body(state):
        turn, rest = state
        sent = pack(turn.reshape(1), plan, matrix)
        got = lax.all_to_all(sent, ROWS, 0, 0)
        return turn + 1, lax.dynamic_update_slice(rest, got[None], (turn - 1, 0, 0, 0))

    rest = blank((NB // SLOTS - 1, N_PROW, 2 * SLOTS, matrix.shape[1]))
    return lax.while_loop(lambda state: state[0] * SLOTS < most, body, (jnp.int32(1), rest))[1]


def local(matrix, pivot_rows):
    zh, x, c = (lax.axis_index(name) for name in COLS)
    zl, y = (lax.axis_index(name) for name in ROWS)
    lower = lax.optimization_barrier(matrix[:NB, :NB])
    targets = ((1, 0), (0, 1), (0, 3))
    received = [send_rows(lower, [((0, 0), t)], [0]) for t in targets]
    plan = make_plan(pivot_rows.reshape(1, NB))
    panel = matrix[:, :NB]
    panel, plan = lax.optimization_barrier((panel, plan))
    *received, plan = lax.optimization_barrier((*received, plan))
    for (a, b), got in zip(targets, received):
        lower = jnp.where((zl == a) & (y == b), got, lower)
    got = send_rows(
        lower, [((0, 0), (0, 2)), ((1, 0), (1, 2)), ((0, 1), (1, 1)), ((0, 3), (1, 3))], [0]
    )
    sent = pack(jnp.zeros((1,), jnp.int32), after(plan, lower), matrix)
    got, sent = lax.optimization_barrier((got, sent))
    lower = jnp.where((y == 2) | ((zl == 1) & (y != 0)), got, lower)
    rows = lax.all_to_all(after(sent, lower), ROWS, 0, 0)
    rest = later_rounds(after(plan, sent), matrix)
    quarters = weigh(lower, panel)

    zs, xs = range(N_ZH), range(N_X)
    to_near = send_cols(quarters[1], [((0, 0, 0), (0, 1, 0))])
    to_far = send_cols(quarters[3], [((0, 0, 0), (0, 3, 1))])
    to_core = send_cols(quarters[2], [((0, 0, 0), (0, 0, 1))])
    piece = jnp.where(
        c == 0, jnp.where(x == 1, to_near, quarters[0]), jnp.where(x == 3, to_far, to_core)
    )
    got = send_cols(
        piece,
        [((0, s, 0), (0, t, 0)) for s, t in ((0, 3), (1, 2))]
        + [((0, s, 1), (0, t, 1)) for s, t in ((0, 1), (3, 2))],
    )
    piece = jnp.where((x == 2) | (x == jnp.where(c == 0, 3, 1)), got, piece)
    upward = (c ^ zl) == 0
    got = send_along_zh(piece, (((0, 1),), ((0, 3),)))
    piece = jnp.where(zh == jnp.where(upward, 1, 3), got, piece)
    base, factors = prepare(plan, after(rows, piece), rest, matrix)
    got = send_along_zh(piece, (((0, 3), (1, 2)), ((0, 1), (3, 2))))
    got = after(got, factors)
    piece = jnp.where((zh == 2) | (zh == jnp.where(upward, 3, 1)), got, piece)
    chips = [(b, a) for a in xs for b in zs]
    swap = [((b, a, d), (b, a, 1 - d)) for b, a in chips for d in (0, 1)]
    across = send_cols(
        piece,
        [((b, a, 0), (b, NEAR[a], 0)) for b, a in chips]
        + [((b, a, 1), (b, FAR[a], 1)) for b, a in chips],
    )
    other = send_cols(piece, swap)
    out = update(True, 0, piece, factors, base, None)
    out = update(False, 0, other, factors, base, out)
    across, out = lax.optimization_barrier((across, out))
    other_across = send_cols(across, swap)
    out = update(True, 1, across, factors, base, out)
    return update(False, 1, other_across, factors, base, out)


def solution(mesh):
    fine = Mesh(mesh.devices.reshape(2, N_Y, N_ZH, N_X, N_C), ROWS + COLS)
    placed = (P(ROWS, COLS), P())
    return jax.shard_map(
        local, mesh=fine, in_specs=placed, out_specs=P(ROWS, COLS), check_vma=False
    )
```

```python
import functools

import jax
import jax.numpy as jnp
from jax import lax
from jax.experimental import pallas as pl
from jax.experimental.pallas import tpu as pltpu
from jax.sharding import Mesh, PartitionSpec as P

NB = 128
EXACT = lax.Precision.HIGHEST
ROWS = ("zl", "y")
COLS = ("zh", "x", "c")
N_Y, N_X, N_ZH, N_C = 4, 4, 4, 2
N_PROW, N_PCOL = 8, 32
N_PART = 4
STEP = NB // N_PROW
SLOTS = 32
BLOCK = 32
PLAN_ROWS = 8

VMEM = pl.BlockSpec(memory_space=pltpu.VMEM)
SMEM = pl.BlockSpec(memory_space=pltpu.SMEM)
ANY = pl.BlockSpec(memory_space=pl.ANY)


SMALL = pltpu.CompilerParams(vmem_limit_bytes=12 << 20)
LARGE = pltpu.CompilerParams(vmem_limit_bytes=56 << 20)


def prow_id(zl, y):
    return zl * N_Y + y


def pcol_id(zh, x, c):
    return (zh * N_X + x) * N_C + c


def my_place():
    row = prow_id(lax.axis_index("zl"), lax.axis_index("y"))
    col = pcol_id(*(lax.axis_index(name) for name in COLS))
    return row, col


NEAR = (1, 0, 3, 2)
FAR = (3, 2, 1, 0)


def send_cols(value, pairs):
    return lax.ppermute(value, COLS, [(pcol_id(*s), pcol_id(*t)) for s, t in pairs])


def send_rows(value, pairs, cols=range(N_PCOL)):
    pairs = [(prow_id(*s) * N_PCOL + q, prow_id(*t) * N_PCOL + q) for s, t in pairs for q in cols]
    return lax.ppermute(value, ROWS + COLS, pairs)


def send_along_zh(value, routes):
    pairs = []
    for zl in range(2):
        for y in range(N_Y):
            for a in range(N_X):
                for d in range(N_C):
                    for s, t in routes[zl ^ d]:
                        row = prow_id(zl, y) * N_PCOL
                        pairs.append((row + pcol_id(s, a, d), row + pcol_id(t, a, d)))
    return lax.ppermute(value, ROWS + COLS, pairs)


def after(value, first):
    return lax.optimization_barrier((value, first))[0]


def owned_row(pivot, my_row):
    is_owned = ((pivot >> 7) & (N_PROW - 1)) == my_row
    return is_owned, jnp.where(is_owned, ((pivot >> 10) << 7) + (pivot & (NB - 1)), 0)


def to_column(row):
    size = row.shape[1]
    rows = lax.broadcasted_iota(jnp.int32, (size, size), 0)
    cols = lax.broadcasted_iota(jnp.int32, (size, size), 1)
    return jnp.sum(jnp.where(rows == cols, row, 0.0), axis=1, keepdims=True)


def ranks_of(pivots):
    owner = ((pivots >> 7) & (N_PROW - 1)).astype(jnp.float32)
    rows = lax.broadcasted_iota(jnp.int32, (NB, NB), 0)
    cols = lax.broadcasted_iota(jnp.int32, (NB, NB), 1)
    before = (to_column(owner) == owner) & (rows < cols)
    return jnp.sum(jnp.where(before, 1.0, 0.0), axis=0, keepdims=True)


def plan_kernel(pivots, out):
    my_row, _ = my_place()
    ranks = ranks_of(pivots[...])
    owner = (pivots[...] >> 7) & (N_PROW - 1)
    is_owned, row = owned_row(pivots[...], my_row)
    rank = to_column(jnp.where(is_owned, ranks, -1.0))
    wanted = lax.broadcasted_iota(jnp.int32, (NB, NB), 1).astype(jnp.float32)
    rows = jnp.where(rank == wanted, to_column(row.astype(jnp.float32)), 0.0)
    count = jnp.sum(is_owned.astype(jnp.float32), axis=1, keepdims=True)
    most = jnp.max(ranks, axis=1, keepdims=True) + 1.0
    out[...] = jnp.zeros_like(out)
    out[0:1, :] = owner * NB + ranks.astype(jnp.int32)
    out[1:2, :] = jnp.sum(rows, axis=0, keepdims=True).astype(jnp.int32)
    out[2:3, :] = jnp.broadcast_to(count, (1, NB)).astype(jnp.int32)
    out[3:4, :] = jnp.broadcast_to(most, (1, NB)).astype(jnp.int32)


def make_plan(pivots):
    return pl.pallas_call(
        plan_kernel,
        out_shape=jax.ShapeDtypeStruct((PLAN_ROWS, NB), jnp.int32),
        in_specs=[VMEM],
        out_specs=VMEM,
        compiler_params=SMALL,
        cost_estimate=pl.CostEstimate(flops=0, bytes_accessed=3 << 20, transcendentals=0),
        name="plan",
    )(pivots)


def pack_kernel(turn, plan, matrix, out, held, top, moved, sem, row_sems, out_sems):
    my_row, _ = my_place()
    on_top = my_row == 0
    load_top = pltpu.make_async_copy(matrix.at[pl.ds(0, NB), :], top, sem)

    @pl.when(on_top)
    def _():
        load_top.start()

    first = turn[0] * SLOTS
    copies = [
        pltpu.make_async_copy(
            matrix.at[pl.ds(plan[1, first + i], 1), :], held.at[pl.ds(i, 1), :], row_sems.at[i]
        )
        for i in range(SLOTS)
    ]
    for copy in copies:
        copy.start()

    def held_copy(j):
        return pltpu.make_async_copy(held, out.at[j, pl.ds(0, SLOTS), :], out_sems.at[j])

    def moved_copy(j):
        return pltpu.make_async_copy(
            moved.at[pl.ds(j * SLOTS, SLOTS), :],
            out.at[j, pl.ds(SLOTS, SLOTS), :],
            out_sems.at[N_PROW + j],
        )

    @pl.when(on_top)
    def _():
        load_top.wait()

        def move(j, _):
            for i in range(8):
                entry = plan[0, j * 8 + i]
                rank = entry & (NB - 1)
                place = ((entry >> 7) << 5) + (rank & (SLOTS - 1))
                place = jnp.where((rank >> 5) == turn[0], place, N_PROW * SLOTS)
                moved[pl.ds(place, 1), :] = top[pl.ds(j * 8 + i, 1), :]
            return 0

        lax.fori_loop(0, NB // 8, move, 0)
        for j in range(N_PROW):
            moved_copy(j).start()

    for copy in copies:
        copy.wait()
    for j in range(N_PROW):
        held_copy(j).start()

    @pl.when(on_top)
    def _():
        for j in range(N_PROW):
            moved_copy(j).wait()

    for j in range(N_PROW):
        held_copy(j).wait()


def pack(turn, plan, matrix):
    cols = matrix.shape[1]
    return pl.pallas_call(
        pack_kernel,
        out_shape=jax.ShapeDtypeStruct((N_PROW, 2 * SLOTS, cols), jnp.float32),
        in_specs=[SMEM, SMEM, ANY],
        out_specs=ANY,
        scratch_shapes=[
            pltpu.VMEM((SLOTS, cols), jnp.float32),
            pltpu.VMEM((NB, cols), jnp.float32),
            pltpu.VMEM(((N_PROW + 1) * SLOTS, cols), jnp.float32),
            pltpu.SemaphoreType.DMA,
            pltpu.SemaphoreType.DMA((SLOTS,)),
            pltpu.SemaphoreType.DMA((2 * N_PROW,)),
        ],
        compiler_params=LARGE,
        cost_estimate=pl.CostEstimate(flops=0, bytes_accessed=6 << 20, transcendentals=0),
        name="pack",
    )(turn, plan, matrix)


def split(value):
    first = value.astype(jnp.bfloat16)
    rest = value - first.astype(jnp.float32)
    second = rest.astype(jnp.bfloat16)
    third = (rest - second.astype(jnp.float32)).astype(jnp.bfloat16)
    return first, second, third


def exact_dot(a, b):
    a1, a2, a3 = split(a)
    b1, b2, b3 = split(b)
    product = functools.partial(jnp.dot, preferred_element_type=jnp.float32)
    lead = jnp.concatenate([a1, a2], axis=1)
    total = product(jnp.concatenate([a1, a3], axis=1), jnp.concatenate([b3, b1], axis=0))
    total = total + product(lead, jnp.concatenate([b2, b2], axis=0))
    return total + product(lead, jnp.concatenate([b1, b1], axis=0))


def inverse_of(lower):
    rows = lax.broadcasted_iota(jnp.int32, (NB, NB), 0)
    cols = lax.broadcasted_iota(jnp.int32, (NB, NB), 1)
    block_bits = BLOCK.bit_length() - 1
    offset = cols - ((rows >> block_bits) << block_bits)
    lower = jnp.where(rows > cols, lower, 0.0)
    inverse = jnp.where(rows == cols, 1.0, 0.0).reshape(NB // BLOCK, BLOCK, NB)
    for j in range(BLOCK - 1):
        column = jnp.sum(jnp.where(offset == j, lower, 0.0), axis=1, keepdims=True)
        column = column.reshape(NB // BLOCK, BLOCK, 1)
        inverse = inverse - column * inverse[:, j : j + 1, :]
    inverse = inverse.reshape(NB, NB)
    size = BLOCK
    while size < NB:
        shift = size.bit_length()
        same = (rows >> shift) == (cols >> shift)
        below = ((rows & size) != 0) & ((cols & size) == 0)
        part = jnp.where(same & below, lower, 0.0)
        inverse = inverse - exact_dot(inverse, exact_dot(part, inverse))
        size *= 2
    return inverse


def weigh_kernel(block, panel_hbm, *refs):
    quarters, (panel, sem) = refs[:N_PART], refs[N_PART:]
    my_row, my_col = my_place()

    @pl.when(my_col == 0)
    def _():
        copy = pltpu.make_async_copy(panel_hbm, panel, sem)
        copy.start()
        inverse = inverse_of(block[...])
        copy.wait()
        height = quarters[0].shape[0]
        for q, out in enumerate(quarters):
            out[...] = exact_dot(panel[q * height : (q + 1) * height, :], inverse)

        @pl.when(my_row == 0)
        def _():
            quarters[0][:NB, :] = -inverse


def weigh(block, panel):
    height = panel.shape[0]
    quarter = jax.ShapeDtypeStruct((height // N_PART, NB), jnp.float32)
    return pl.pallas_call(
        weigh_kernel,
        out_shape=(quarter,) * N_PART,
        in_specs=[VMEM, ANY],
        out_specs=(VMEM,) * N_PART,
        scratch_shapes=[pltpu.VMEM((height, NB), jnp.float32), pltpu.SemaphoreType.DMA],
        compiler_params=SMALL,
        name="weigh",
    )(block, panel)


def prepare_kernel(plan_hbm, rows, rest, matrix, base, factors, picked, own, plan, sems):
    my_row, my_col = my_place()
    load = pltpu.make_async_copy(plan_hbm, plan, sems.at[0])
    whole = pltpu.make_async_copy(matrix, base, sems.at[1])
    load.start()
    whole.start()
    load.wait()

    def find(j, _):
        for i in range(8):
            k = j * 8 + i
            entry = plan[0, k]
            place = entry & (SLOTS - 1)
            picked[pl.ds(k, 1), :] = rows[entry >> 7, pl.ds(place, 1), :]
        return 0

    lax.fori_loop(0, NB // 8, find, 0)

    def fetch(turn, source, place, target):
        copy = pltpu.make_async_copy(
            rest.at[turn - 1, source, pl.ds(place, 1), :], target, sems.at[0]
        )
        copy.start()
        copy.wait()

    @pl.when(plan[3, 0] > SLOTS)
    def _():
        def find_late(k, _):
            entry = plan[0, k]
            rank = entry & (NB - 1)

            @pl.when(rank >= SLOTS)
            def _():
                fetch(rank >> 5, entry >> 7, rank & (SLOTS - 1), picked.at[pl.ds(k, 1), :])

            return 0

        lax.fori_loop(0, NB, find_late, 0)

    first, second, third = split(picked[...])
    factors[0, :NB, :] = first
    factors[0, NB:, :] = first
    factors[1, :NB, :] = second
    factors[1, NB:, :] = second
    factors[2, :NB, :] = third
    factors[2, NB:, :] = first
    whole.wait()

    @pl.when(my_col == 0)
    def _():
        own[...] = base[:, :NB]

    def swap(i, _):
        base[pl.ds(plan[1, i], 1), :] = rows[0, pl.ds(SLOTS + i, 1), :]
        return 0

    lax.fori_loop(0, jnp.minimum(plan[2, 0], SLOTS), swap, 0)

    def swap_late(i, _):
        place = SLOTS + (i & (SLOTS - 1))
        fetch(i >> 5, 0, place, base.at[pl.ds(plan[1, i], 1), :])
        return 0

    lax.fori_loop(SLOTS, jnp.maximum(plan[2, 0], SLOTS), swap_late, 0)

    @pl.when(my_row == 0)
    def _():
        base[:NB, :] = jnp.zeros((NB, base.shape[1]), jnp.float32)

    @pl.when(my_col == 0)
    def _():
        base[:, :NB] = own[...]
        factors[:, :, :NB] = jnp.zeros((3, 2 * NB, NB), jnp.bfloat16)


def prepare(plan, rows, rest, matrix):
    height, cols = matrix.shape
    return pl.pallas_call(
        prepare_kernel,
        out_shape=(
            jax.ShapeDtypeStruct(matrix.shape, jnp.float32),
            jax.ShapeDtypeStruct((3, 2 * NB, cols), jnp.bfloat16),
        ),
        in_specs=[ANY, VMEM, ANY, ANY],
        out_specs=(VMEM, VMEM),
        scratch_shapes=[
            pltpu.VMEM((NB, cols), jnp.float32),
            pltpu.VMEM((height, NB), jnp.float32),
            pltpu.SMEM((PLAN_ROWS, NB), jnp.int32),
            pltpu.SemaphoreType.DMA((2,)),
        ],
        compiler_params=SMALL,
        cost_estimate=pl.CostEstimate(flops=0, bytes_accessed=9 << 20, transcendentals=0),
        name="prepare",
    )(plan, rows, rest, matrix)


def holdings():
    x, c = lax.axis_index("x"), lax.axis_index("c")
    bits = ((x == 1) | (x == 2)).astype(jnp.int32), (x >= 2).astype(jnp.int32)
    mine = jnp.where(c == 0, bits[0], bits[1])
    other = jnp.where(c == 0, bits[1], bits[0])
    return c, mine, other


def update_kernel(mine, late, piece, factors, base, *refs):
    out, buffer, sem = refs[-3:]
    core, my_bit, other_bit = holdings()
    height = piece.shape[0]
    quarter = 2 * core + (my_bit ^ late) if mine else 2 * (1 - core) + (other_bit ^ late)
    start = pl.multiple_of(quarter * height, height)
    first, second, third = split(piece[...])
    lead = jnp.concatenate([first, second], axis=1)
    tail = jnp.concatenate([first, third], axis=1)
    product = functools.partial(jnp.dot, preferred_element_type=jnp.float32)
    total = product(tail, factors[2]) + product(lead, factors[1]) + product(lead, factors[0])
    buffer[...] = base[pl.ds(start, height), :] - total
    copy = pltpu.make_async_copy(buffer, out.at[pl.ds(start, height), :], sem)
    copy.start()
    copy.wait()


def update(mine, late, piece, factors, base, done):
    height, cols = piece.shape[0], base.shape[1]
    extra = [] if done is None else [done]
    return pl.pallas_call(
        functools.partial(update_kernel, mine, late),
        out_shape=jax.ShapeDtypeStruct(base.shape, jnp.float32),
        in_specs=[VMEM] * 3 + [ANY] * len(extra),
        out_specs=ANY,
        scratch_shapes=[pltpu.VMEM((height, cols), jnp.float32), pltpu.SemaphoreType.DMA],
        input_output_aliases={3: 0} if extra else {},
        compiler_params=SMALL,
        cost_estimate=pl.CostEstimate(flops=0, bytes_accessed=2 << 20, transcendentals=0),
        name="update",
    )(piece, factors, base, *extra)


def blank_kernel(out):
    pass


def blank(shape):
    return pl.pallas_call(
        blank_kernel,
        out_shape=jax.ShapeDtypeStruct(shape, jnp.float32),
        out_specs=ANY,
        compiler_params=SMALL,
        name="blank",
    )()


def later_rounds(plan, matrix):
    most = plan[3, 0]

    def body(state):
        turn, rest = state
        sent = pack(turn.reshape(1), plan, matrix)
        got = lax.all_to_all(sent, ROWS, 0, 0)
        return turn + 1, lax.dynamic_update_slice(rest, got[None], (turn - 1, 0, 0, 0))

    rest = blank((NB // SLOTS - 1, N_PROW, 2 * SLOTS, matrix.shape[1]))
    return lax.while_loop(lambda state: state[0] * SLOTS < most, body, (jnp.int32(1), rest))[1]


def local(matrix, pivot_rows):
    zh, x, c = (lax.axis_index(name) for name in COLS)
    zl, y = (lax.axis_index(name) for name in ROWS)
    lower = lax.optimization_barrier(matrix[:NB, :NB])
    targets = ((0, 3), (0, 1), (1, 0))
    received = [send_rows(lower, [((0, 0), t)], [0]) for t in targets]
    plan = make_plan(pivot_rows.reshape(1, NB))
    panel = matrix[:, :NB]
    panel, plan = lax.optimization_barrier((panel, plan))
    *received, plan = lax.optimization_barrier((*received, plan))
    for (a, b), got in zip(targets, received):
        lower = jnp.where((zl == a) & (y == b), got, lower)
    got = send_rows(
        lower, [((0, 0), (0, 2)), ((1, 0), (1, 2)), ((0, 1), (1, 1)), ((0, 3), (1, 3))], [0]
    )
    sent = pack(jnp.zeros((1,), jnp.int32), after(plan, lower), matrix)
    got, sent = lax.optimization_barrier((got, sent))
    lower = jnp.where((y == 2) | ((zl == 1) & (y != 0)), got, lower)
    rows = lax.all_to_all(after(sent, lower), ROWS, 0, 0)
    rest = later_rounds(after(plan, sent), matrix)
    quarters = weigh(lower, panel)

    zs, xs = range(N_ZH), range(N_X)
    to_near = send_cols(quarters[1], [((0, 0, 0), (0, 1, 0))])
    to_far = send_cols(quarters[3], [((0, 0, 0), (0, 3, 1))])
    to_core = send_cols(quarters[2], [((0, 0, 0), (0, 0, 1))])
    piece = jnp.where(
        c == 0, jnp.where(x == 1, to_near, quarters[0]), jnp.where(x == 3, to_far, to_core)
    )
    got = send_cols(
        piece,
        [((0, s, 0), (0, t, 0)) for s, t in ((0, 3), (1, 2))]
        + [((0, s, 1), (0, t, 1)) for s, t in ((0, 1), (3, 2))],
    )
    piece = jnp.where((x == 2) | (x == jnp.where(c == 0, 3, 1)), got, piece)
    upward = (c ^ zl) == 0
    got = send_along_zh(piece, (((0, 1),), ((0, 3),)))
    piece = jnp.where(zh == jnp.where(upward, 1, 3), got, piece)
    base, factors = prepare(plan, after(rows, piece), rest, matrix)
    got = send_along_zh(piece, (((0, 3), (1, 2)), ((0, 1), (3, 2))))
    got = after(got, factors)
    piece = jnp.where((zh == 2) | (zh == jnp.where(upward, 3, 1)), got, piece)
    chips = [(b, a) for a in xs for b in zs]
    swap = [((b, a, d), (b, a, 1 - d)) for b, a in chips for d in (0, 1)]
    across = send_cols(
        piece,
        [((b, a, 0), (b, NEAR[a], 0)) for b, a in chips]
        + [((b, a, 1), (b, FAR[a], 1)) for b, a in chips],
    )
    other = send_cols(piece, swap)
    out = update(True, 0, piece, factors, base, None)
    out = update(False, 0, other, factors, base, out)
    across, out = lax.optimization_barrier((across, out))
    other_across = send_cols(across, swap)
    out = update(True, 1, across, factors, base, out)
    return update(False, 1, other_across, factors, base, out)


def solution(mesh):
    fine = Mesh(mesh.devices.reshape(2, N_Y, N_ZH, N_X, N_C), ROWS + COLS)
    placed = (P(ROWS, COLS), P())
    return jax.shard_map(
        local, mesh=fine, in_specs=placed, out_specs=P(ROWS, COLS), check_vma=False
    )
```
